32 devices in a mesh: region: 2 (over y), row: 2 (over core), col: 8 (over z, x).
Axes of the slice: x: 2, y: 2, z: 4, core: 2. Of those that a mesh axis runs over, the one named last changes fastest.
Arguments:
- blocks: bfloat16 [4, 8, 128, 128, 128], P(('region', 'row'), 'col'), parts along dimension 0, may hold values from -0.125 to 0.125
- block_rows: int32 [4, 8, 128], P(('region', 'row'), 'col'), parts along dimension 0, may hold values from 0 to 63, as said below
- block_cols: int32 [4, 8, 128], P(('region', 'row'), 'col'), parts along dimension 0, may hold values from 0 to 7, as said below
- counts: int32 [4, 8], P(('region', 'row'), 'col'), parts along dimension 0, may hold values from 42 to 128, as said below
- u_rays: float32 [8, 32768], P(None, ('region', 'row', 'col')), parts along dimension 1, may hold values from -6 to 6
- v_cells: float32 [8, 16384], P(None, ('region', 'col', 'row')), parts along dimension 1, may hold values from -6 to 6
- x_cells: float32 [8, 16384], P(None, ('region', 'col', 'row')), parts along dimension 1, may hold values from -6 to 6
- w_cells: float32 [8, 16384], P(None, ('region', 'col', 'row')), parts along dimension 1, may hold values from -6 to 6
- alpha: float32 [16], P('region'), parts along dimension 0, may hold values from 0.5 to 2
- phibar: float32 [16], P('region'), parts along dimension 0, may hold values from 0.5 to 2
- rhobar: float32 [16], P('region'), parts along dimension 0, may hold values from 0.5 to 2
Outputs:
- u_next: float32 [8, 32768], P(None, ('region', 'row', 'col')), parts along dimension 1
- v_next: float32 [8, 16384], P(None, ('region', 'col', 'row')), parts along dimension 1
- x_next: float32 [8, 16384], P(None, ('region', 'col', 'row')), parts along dimension 1
- w_next: float32 [8, 16384], P(None, ('region', 'col', 'row')), parts along dimension 1
- scalars: float32 [3, 16], P(None, 'region'), parts along dimension 1
The draws below stay inside these ranges and needn't reach their ends.
There are 2 independent parts, one for each index of `region`. The reference program is written for one: setup_inputs(seed, part) draws one part's arguments, and reference() takes and returns one part's arrays. A program takes and returns all parts, laid end to end along the dimension named above; each array names one. Nothing has to cross between parts.
Inputs may be any that keep to these rules, and one draw needn't show every extreme that they name: Block row within the row group, below 64; the pairs (block_rows, block_cols) of one device's slots are all different. `block_cols`: block column within the column group, below 8. Only slots k < counts of a device hold blocks of A; the values in the other slots are not part of A.
All inputs are finite; a program needn't handle non-finite values.
Results may differ from the reference program's by a relative error of at most 0.015.
Values may be sent and summed in bfloat16 or wider, within the bound.
No kernel may reach another device: no remote copies, remote signals or barrier semaphores. Data moves between devices by JAX's collectives and lax.ppermute only.
A program may use at most 64 MiB of HBM per device.

```python
import math
import jax
import jax.numpy as jnp
from jax import lax

RHS = 8
BLK = 128
BR_DEV = 64
BC_DEV = 8
NB_DEV = 128
ITERS = 2
GROUP_ROWS = 2
GROUP_COLS = 8
RAYS = 16384
CELLS = 8192


def coverage(key):
    keys = jax.random.split(key, GROUP_ROWS * GROUP_COLS)
    perms = jax.vmap(lambda k: jax.random.permutation(k, BR_DEV * BC_DEV)[:NB_DEV])(keys)
    return perms.reshape(GROUP_ROWS, GROUP_COLS, NB_DEV).astype(jnp.int32)


def draw_block_rows(key, part):
    picked = coverage(key)
    return picked // BC_DEV


def draw_block_cols(key, part):
    picked = coverage(key)
    return picked % BC_DEV


def draw_counts(key, part):
    key = jax.random.fold_in(key, 7)
    column = jnp.arange(GROUP_COLS, dtype=jnp.int32)
    lowest = NB_DEV // 3 + (NB_DEV - NB_DEV // 3) * column // (GROUP_COLS - 1)
    spread = NB_DEV - lowest + 1
    extra = jax.random.randint(key, (GROUP_ROWS, GROUP_COLS), 0, 65536, dtype=jnp.int32) % spread[None, :]
    return (lowest[None, :] + extra).astype(jnp.int32)


def steps_of(key, dims, cuts, least, largest):
    loudness = 1.0
    for position, blocks in cuts:
        heights = jax.random.uniform(jax.random.fold_in(jax.random.fold_in(key, 6), position), (blocks,), jnp.float32, least / len(cuts), largest / len(cuts))
        loudness = loudness * jnp.repeat(jnp.exp(heights), dims[position] // blocks).reshape((-1,) + (1,) * (len(dims) - 1 - position))
    return loudness


def normal_values(key, shape, deviation, reach, shards=(), kind=jnp.bfloat16):
    loudness = steps_of(key, shape, shards, -0.22, 0.18) if shards else 1.0
    values = jax.random.normal(key, shape, jnp.float32) * deviation * loudness
    return jnp.minimum(jnp.maximum(values, -reach), reach).astype(kind)


def setup_inputs(seed: int = 0, part: int = 0) -> dict:
    seeds = jax.random.split(jax.random.key(seed), 12)
    part_splits = jax.random.split(jax.random.fold_in(seeds[11], part), 12)
    blocks = normal_values(part_splits[0], (GROUP_ROWS, GROUP_COLS, NB_DEV, BLK, BLK), (BLK * NB_DEV * GROUP_COLS // BR_DEV) ** -0.5, 0.125, ((0, 2), (1, 8)))
    block_rows = draw_block_rows(jax.random.fold_in(jax.random.fold_in(seeds[11], part), 71), part)
    block_cols = draw_block_cols(jax.random.fold_in(jax.random.fold_in(seeds[11], part), 71), part)
    counts = draw_counts(jax.random.fold_in(jax.random.fold_in(seeds[11], part), 71), part)
    u_rays = normal_values(part_splits[4], (RHS, RAYS), 1.0, 6.0, ((1, 16),), jnp.float32)
    v_cells = normal_values(part_splits[5], (RHS, CELLS), 1.0, 6.0, ((1, 16),), jnp.float32)
    x_cells = normal_values(part_splits[6], (RHS, CELLS), 1.0, 6.0, ((1, 16),), jnp.float32)
    w_cells = normal_values(part_splits[7], (RHS, CELLS), 1.0, 6.0, ((1, 16),), jnp.float32)
    alpha = jnp.clip(jnp.exp(jax.random.uniform(part_splits[8], (RHS,), jnp.float32, math.log(0.5), math.log(2.0))), 0.5, 2.0)
    phibar = jnp.clip(jnp.exp(jax.random.uniform(part_splits[9], (RHS,), jnp.float32, math.log(0.5), math.log(2.0))), 0.5, 2.0)
    rhobar = jnp.clip(jnp.exp(jax.random.uniform(part_splits[10], (RHS,), jnp.float32, math.log(0.5), math.log(2.0))), 0.5, 2.0)
    return dict(blocks=blocks, block_rows=block_rows, block_cols=block_cols, counts=counts, u_rays=u_rays, v_cells=v_cells, x_cells=x_cells, w_cells=w_cells, alpha=alpha, phibar=phibar, rhobar=rhobar)


HI = lax.Precision.HIGHEST

def local_forward(blk, rws, cls, cnt, vg3):
    sel = jnp.take(vg3, cls, axis=1).astype(jnp.float32)
    prod = jnp.einsum('skj,kij->ski', sel, blk.astype(jnp.float32), precision=HI)
    mask = (jnp.arange(blk.shape[0]) < cnt).astype(jnp.float32)
    onehot = (rws[:, None] == jnp.arange(BR_DEV)[None, :]).astype(jnp.float32) * mask[:, None]
    out = jnp.einsum('kb,ski->sbi', onehot, prod, precision=HI)
    return out.reshape(RHS, BR_DEV * BLK)

def local_backward(blk, rws, cls, cnt, ug3):
    sel = jnp.take(ug3, rws, axis=1).astype(jnp.float32)
    prod = jnp.einsum('ski,kij->skj', sel, blk.astype(jnp.float32), precision=HI)
    mask = (jnp.arange(blk.shape[0]) < cnt).astype(jnp.float32)
    onehot = (cls[:, None] == jnp.arange(BC_DEV)[None, :]).astype(jnp.float32) * mask[:, None]
    out = jnp.einsum('kb,skj->sbj', onehot, prod, precision=HI)
    return out.reshape(RHS, BC_DEV * BLK)

def reference(blocks, block_rows, block_cols, counts, u_rays, v_cells, x_cells, w_cells, alpha, phibar, rhobar):
    u, v, x, w = (u_rays, v_cells, x_cells, w_cells)
    col_width = BC_DEV * BLK
    for step in range(ITERS):
        vb = v.astype(jnp.bfloat16)
        groups = []
        for grp in range(GROUP_ROWS):

            def add_col(total, items):
                blk, rws, cls, cnt, idx = items
                piece = lax.dynamic_slice_in_dim(vb, (idx * col_width).astype(jnp.int32), col_width, 1)
                return (total + local_forward(blk, rws, cls, cnt, piece.reshape(RHS, BC_DEV, BLK)), None)
            start = jnp.zeros((RHS, BR_DEV * BLK), jnp.float32)
            total, unused = lax.scan(add_col, start, (blocks[grp], block_rows[grp], block_cols[grp], counts[grp], jnp.arange(GROUP_COLS, dtype=jnp.int32)))
            groups.append(total)
        upd = jnp.concatenate(groups, axis=1) - alpha[:, None] * u
        beta = jnp.sqrt(lax.optimization_barrier(jnp.mean(upd * upd, axis=1)) + 1e-06)
        u = upd / beta[:, None]
        ub = u.astype(jnp.bfloat16)
        vsum = jnp.zeros((RHS, GROUP_COLS, col_width), jnp.float32)
        for grp in range(GROUP_ROWS):
            ug3 = ub[:, grp * BR_DEV * BLK:(grp + 1) * BR_DEV * BLK].reshape(RHS, BR_DEV, BLK)

            def one_col(items):
                blk, rws, cls, cnt = items
                return local_backward(blk, rws, cls, cnt, ug3)
            parts_out = lax.map(one_col, (blocks[grp], block_rows[grp], block_cols[grp], counts[grp]))
            vsum = vsum + jnp.transpose(parts_out, (1, 0, 2))
        vupd = vsum.reshape(RHS, GROUP_COLS * col_width) - beta[:, None] * v
        alpha = jnp.sqrt(lax.optimization_barrier(jnp.mean(vupd * vupd, axis=1)) + 1e-06)
        v = vupd / alpha[:, None]
        rho = jnp.sqrt(rhobar * rhobar + beta * beta)
        cosine = rhobar / rho
        sine = beta / rho
        theta = sine * alpha
        phi = cosine * phibar
        rhobar = -cosine * alpha
        phibar = sine * phibar
        x = x + (phi / rho)[:, None] * w
        w = v - (theta / rho)[:, None] * w
    return (u, v, x, w, jnp.stack([alpha, phibar, rhobar]))
```

```python
import functools

import jax
import jax.numpy as jnp
from jax import lax
from jax.experimental import pallas as pl
from jax.experimental.pallas import tpu as pltpu
from jax.sharding import PartitionSpec as P

ITERS = 2
EPS = 1e-6
UNROLL = 4
F32 = jnp.float32
BF16 = jnp.bfloat16
SMEM = pl.BlockSpec(memory_space=pltpu.SMEM)
VMEM = pl.BlockSpec(memory_space=pltpu.VMEM)


def call(kernel, out_shape, in_specs, scratch=()):
    return pl.pallas_call(
        kernel,
        out_shape=out_shape,
        in_specs=in_specs,
        out_specs=jax.tree.map(lambda _: VMEM, out_shape),
        scratch_shapes=list(scratch),
        compiler_params=pltpu.CompilerParams(vmem_limit_bytes=48 * 1024 * 1024),
    )


def shape(*dims, dtype=F32):
    return jax.ShapeDtypeStruct(dims, dtype)


def forward(blk, rws, cls, cnt, v_ref, acc_ref):
    spare = acc_ref.shape[0] - 1
    count = cnt[0, 0]
    acc_ref[...] = jnp.zeros_like(acc_ref)

    def group(g, carry):
        prods = []
        for p in range(UNROLL):
            k = (g * UNROLL + p) * 2
            pair = jnp.concatenate([v_ref[cls[0, 0, k]], v_ref[cls[0, 0, k + 1]]], axis=0)
            a = blk[0, 0, pl.ds(k, 2)].reshape(256, 128)
            prods.append(
                lax.dot_general(
                    pair.astype(BF16), a, (((1,), (1,)), ((), ())), preferred_element_type=F32
                )
            )
        for p in range(UNROLL):
            k = (g * UNROLL + p) * 2
            r0 = jnp.where(k < count, rws[0, 0, k], spare)
            acc_ref[r0] += prods[p][:8, :128]
            r1 = jnp.where(k + 1 < count, rws[0, 0, k + 1], spare)
            acc_ref[r1] += prods[p][8:, 128:]
        return carry

    step = 2 * UNROLL
    lax.fori_loop(0, (count + step - 1) // step, group, 0)


def backward(blk, rws, cls, cnt, u_ref, acc_ref):
    spare = acc_ref.shape[0] - 1
    count = cnt[0, 0]
    acc_ref[...] = jnp.zeros_like(acc_ref)
    zero = jnp.zeros((8, 128), F32)

    def group(g, carry):
        prods = []
        for p in range(UNROLL):
            k = (g * UNROLL + p) * 2
            u0 = jnp.concatenate([u_ref[rws[0, 0, k]], zero], axis=0).astype(BF16)
            u1 = jnp.concatenate([zero, u_ref[rws[0, 0, k + 1]]], axis=0).astype(BF16)
            pair = jnp.concatenate([u0, u1], axis=1)
            a = blk[0, 0, pl.ds(k, 2)].reshape(256, 128)
            prods.append(jnp.dot(pair, a, preferred_element_type=F32))
        for p in range(UNROLL):
            k = (g * UNROLL + p) * 2
            c0 = jnp.where(k < count, cls[0, 0, k], spare)
            acc_ref[c0] += prods[p][:8]
            c1 = jnp.where(k + 1 < count, cls[0, 0, k + 1], spare)
            acc_ref[c1] += prods[p][8:]
        return carry

    step = 2 * UNROLL
    lax.fori_loop(0, (count + step - 1) // step, group, 0)


def column(ref):
    rows = lax.broadcasted_iota(jnp.int32, (8, 128), 0)
    out = jnp.zeros((8, 128), F32)
    for s in range(8):
        out = jnp.where(rows == s, ref[s], out)
    return out


def lane_sum(x):
    return jnp.broadcast_to(jnp.sum(x, axis=1, keepdims=True), (8, 128))


def squares(ref, blocks):
    total = jnp.zeros((8, 128), F32)
    for b in range(blocks):
        total = total + ref[b] * ref[b]
    return lane_sum(total)


def store_pairs(acc_ref, out_ref, blocks):
    for b in range(0, blocks, 2):
        pair = jnp.concatenate([acc_ref[b], acc_ref[b + 1]], axis=0)
        out_ref[b // 2] = pair.astype(BF16)


def place_halves(own, other, out_ref):
    half = own.shape[1] // 128
    row = lax.axis_index("row")
    for b in range(half):
        out_ref[row * half + b] = own[:, b * 128 : (b + 1) * 128]
        out_ref[(1 - row) * half + b] = other[:, b * 128 : (b + 1) * 128]


def first_forward(rws, cls, cnt, alpha, blk, own, other, u_piece, out, v_out, acc):
    place_halves(own, other, v_out)
    forward(blk, rws, cls, cnt, v_out, acc)
    pieces = u_piece.shape[1] // 128
    base = lax.axis_index("col") * pieces
    a = column(alpha)
    for b in range(pieces):
        acc[base + b] -= a * u_piece[:, b * 128 : (b + 1) * 128]
    store_pairs(acc, out, acc.shape[0] - 1)


def first_backward(rws, cls, cnt, blk, sum0, sum1, upd, message, acc):
    blocks = upd.shape[0]
    for b in range(blocks // 2):
        s = sum0[b].astype(F32) + sum1[b].astype(F32)
        upd[2 * b] = s[:8]
        upd[2 * b + 1] = s[8:]
    backward(blk, rws, cls, cnt, upd, acc)
    cells = acc.shape[0] - 1
    message[:cells] = acc[:cells]
    message[cells] = squares(upd, blocks)


def next_forward(total_rays, rws, cls, cnt, blk, own, other, v_old, out, vupd, beta_out, acc):
    cells = v_old.shape[0]
    beta = jnp.sqrt((own[cells] + other[cells]) / total_rays + EPS)
    beta_out[...] = beta
    inv = 1.0 / beta
    for b in range(cells):
        vupd[b] = (own[b] + other[b]) * inv - beta * v_old[b]
    forward(blk, rws, cls, cnt, vupd, acc)
    rays = acc.shape[0] - 1
    store_pairs(acc, out, rays)
    sq = squares(vupd, cells)
    lanes = lax.broadcasted_iota(jnp.int32, (8, 128), 1)
    sq = jnp.where(lanes == lax.axis_index("col"), sq, 0.0)
    high = sq.astype(BF16).astype(F32)
    out[rays // 2] = jnp.concatenate([high, sq - high], axis=0).astype(BF16)


def next_backward(
    total_cells, pieces, rws, cls, cnt, blk, sum0, sum1, old, beta, message, u_piece, alpha_out, upd, acc
):
    blocks = upd.shape[0]
    tail = sum0[blocks // 2].astype(F32) + sum1[blocks // 2].astype(F32)
    alpha = jnp.sqrt(lane_sum(tail[:8] + tail[8:]) / total_cells + EPS)
    alpha_out[...] = alpha
    inv = 1.0 / alpha
    ratio = alpha / beta[...]
    for b in range(blocks // 2):
        s = sum0[b].astype(F32) + sum1[b].astype(F32)
        upd[2 * b] = s[:8] * inv - ratio * old[2 * b]
        upd[2 * b + 1] = s[8:] * inv - ratio * old[2 * b + 1]
    backward(blk, rws, cls, cnt, upd, acc)
    cells = acc.shape[0] - 1
    message[:cells] = acc[:cells]
    message[cells] = squares(upd, blocks)
    base = lax.axis_index("col") * pieces
    for b in range(pieces):
        u_piece[b] = upd[base + b]


def last_cells(total_rays, own, other, v_old, alpha, sq_out, vupd, beta_out):
    cells = v_old.shape[0]
    beta = jnp.sqrt((own[cells] + other[cells]) / total_rays + EPS)
    beta_out[...] = beta
    inv = 1.0 / beta
    scale = beta / alpha[...]
    for b in range(cells):
        vupd[b] = (own[b] + other[b]) * inv - scale * v_old[b]
    sq = squares(vupd, cells)
    for c in range(sq_out.shape[0]):
        sq_out[c] = sq


def finish(
    total_cells,
    phibar_in,
    rhobar_in,
    sq,
    v1,
    v2,
    u_piece,
    x_in,
    w_in,
    beta1,
    alpha1,
    beta2,
    u_out,
    v_out,
    x_out,
    w_out,
    scalars,
):
    total = sq[0]
    for c in range(1, sq.shape[0]):
        total = total + sq[c]
    alpha2 = jnp.sqrt(total / total_cells + EPS)
    phibar, rhobar = column(phibar_in), column(rhobar_in)
    steps = []
    for beta, alpha in ((beta1[...], alpha1[...]), (beta2[...], alpha2)):
        rho = jnp.sqrt(rhobar * rhobar + beta * beta)
        cosine, sine = rhobar / rho, beta / rho
        steps.append((cosine * phibar / rho, sine * alpha / rho, 1.0 / alpha))
        rhobar = -cosine * alpha
        phibar = sine * phibar
    half = x_in.shape[1] // 128
    base = lax.axis_index("row") * half
    for b in range(half):
        at = slice(b * 128, (b + 1) * 128)
        x, w = x_in[:, at], w_in[:, at]
        for (along, back, inv), vupd in zip(steps, (v1, v2)):
            v = vupd[base + b] * inv
            x = x + along * w
            w = v - back * w
        v_out[:, at], x_out[:, at], w_out[:, at] = v, x, w
    inv = 1.0 / beta2[...]
    for b in range(u_piece.shape[0]):
        u_out[:, b * 128 : (b + 1) * 128] = u_piece[b] * inv
    rows = lax.broadcasted_iota(jnp.int32, (8, 128), 0)
    lanes = lax.broadcasted_iota(jnp.int32, (8, 128), 1)
    for i, value in enumerate((alpha2, phibar, rhobar)):
        line = jnp.sum(jnp.where(rows == lanes, value, 0.0), axis=0, keepdims=True)
        scalars[i : i + 1, :] = line[:, :8]


def other_core(x):
    return lax.ppermute(x, "row", [(0, 1), (1, 0)])


def column_sum(x):
    n = lax.axis_size("col")
    m = 1
    while True:
        y = lax.ppermute(x, "col", [(i, i ^ m) for i in range(n)])
        m *= 2
        if m >= n:
            return x, y
        x = (x.astype(F32) + y.astype(F32)).astype(BF16)


def body(
    blocks, block_rows, block_cols, counts, u_rays, v_cells, x_cells, w_cells, alpha, phibar, rhobar
):
    n_row = lax.axis_size("row")
    n_col = lax.axis_size("col")
    pieces = u_rays.shape[1] // 128
    half = v_cells.shape[1] // 128
    rays = pieces * n_col
    cells = half * n_row
    total_rays = float(rays * 128 * n_row)
    total_cells = float(cells * 128 * n_col)
    where = (block_rows, block_cols, counts)
    listed = [SMEM] * 3
    ray_acc = pltpu.VMEM((rays + 1, 8, 128), F32)
    cell_acc = pltpu.VMEM((cells + 1, 8, 128), F32)

    part, v0 = call(
        first_forward,
        (shape(rays // 2, 16, 128, dtype=BF16), shape(cells, 8, 128)),
        listed + [SMEM] + [VMEM] * 4,
        [ray_acc],
    )(*where, alpha, blocks, v_cells, other_core(v_cells), u_rays)
    sum0, sum1 = column_sum(part)
    upd1, message = call(
        first_backward,
        (shape(rays, 8, 128), shape(cells + 1, 8, 128)),
        listed + [VMEM] * 3,
        [cell_acc],
    )(*where, blocks, sum0, sum1)
    part, v1, beta1 = call(
        functools.partial(next_forward, total_rays),
        (shape(rays // 2 + 1, 16, 128, dtype=BF16), shape(cells, 8, 128), shape(8, 128)),
        listed + [VMEM] * 4,
        [ray_acc],
    )(*where, blocks, message, other_core(message), v0)
    sum0, sum1 = column_sum(part)
    message, u_piece, alpha1 = call(
        functools.partial(next_backward, total_cells, pieces),
        (shape(cells + 1, 8, 128), shape(pieces, 8, 128), shape(8, 128)),
        listed + [VMEM] * 5,
        [pltpu.VMEM((rays, 8, 128), F32), cell_acc],
    )(*where, blocks, sum0, sum1, upd1, beta1)
    sq, v2, beta2 = call(
        functools.partial(last_cells, total_rays),
        (shape(n_col, 8, 128), shape(cells, 8, 128), shape(8, 128)),
        [VMEM] * 4,
    )(message, other_core(message), v1, alpha1)
    sq = lax.all_to_all(sq, "col", 0, 0, tiled=True)
    flat = shape(*v_cells.shape)
    return call(
        functools.partial(finish, total_cells),
        (shape(*u_rays.shape), flat, flat, flat, shape(3, 8)),
        [SMEM] * 2 + [VMEM] * 9,
    )(phibar, rhobar, sq, v1, v2, u_piece, x_cells, w_cells, beta1, alpha1, beta2)


def solution(mesh):
    placed = (
        P(("region", "row"), "col", None, None, None),
        P(("region", "row"), "col", None),
        P(("region", "row"), "col", None),
        P(("region", "row"), "col"),
        P(None, ("region", "row", "col")),
        P(None, ("region", "col", "row")),
        P(None, ("region", "col", "row")),
        P(None, ("region", "col", "row")),
        P("region"),
        P("region"),
        P("region"),
    )
    return jax.shard_map(
        body,
        mesh=mesh,
        in_specs=placed,
        out_specs=(
            P(None, ("region", "row", "col")),
            P(None, ("region", "col", "row")),
            P(None, ("region", "col", "row")),
            P(None, ("region", "col", "row")),
            P(None, "region"),
        ),
        check_vma=False,
    )
```

```python
import functools

import jax
import jax.numpy as jnp
from jax import lax
from jax.experimental import pallas as pl
from jax.experimental.pallas import tpu as pltpu
from jax.sharding import PartitionSpec as P

ITERS = 2
EPS = 1e-6
F32 = jnp.float32
BF16 = jnp.bfloat16
SMEM = pl.BlockSpec(memory_space=pltpu.SMEM)
HBM = pl.BlockSpec(memory_space=pltpu.HBM)
VMEM = pl.BlockSpec(memory_space=pltpu.VMEM)


def call(kernel, out_shape, in_specs, scratch=()):
    return pl.pallas_call(
        kernel,
        out_shape=out_shape,
        in_specs=in_specs,
        out_specs=jax.tree.map(lambda _: VMEM, out_shape),
        scratch_shapes=list(scratch),
        compiler_params=pltpu.CompilerParams(vmem_limit_bytes=48 * 1024 * 1024),
    )


def shape(*dims, dtype=F32):
    return jax.ShapeDtypeStruct(dims, dtype)


def forward(blk, rws, cls, cnt, v_ref, acc_ref, ready=None):
    spare = acc_ref.shape[0] - 1
    count = cnt[0, 0]
    acc_ref[...] = jnp.zeros_like(acc_ref)
    for k in range(0, blk.shape[0], 2):
        if ready is not None:
            ready(k)
        pair = jnp.concatenate([v_ref[cls[0, 0, k]], v_ref[cls[0, 0, k + 1]]], axis=0)
        a = blk[k : k + 2].reshape(256, 128)
        prod = lax.dot_general(
            pair.astype(BF16), a, (((1,), (1,)), ((), ())), preferred_element_type=F32
        )
        acc_ref[jnp.where(k < count, rws[0, 0, k], spare)] += prod[:8, :128]
        acc_ref[jnp.where(k + 1 < count, rws[0, 0, k + 1], spare)] += prod[8:, 128:]


def backward(blk, rws, cls, cnt, u_ref, acc_ref):
    spare = acc_ref.shape[0] - 1
    count = cnt[0, 0]
    acc_ref[...] = jnp.zeros_like(acc_ref)
    zero = jnp.zeros((8, 128), F32)
    for k in range(0, blk.shape[0], 2):
        u0 = jnp.concatenate([u_ref[rws[0, 0, k]], zero], axis=0).astype(BF16)
        u1 = jnp.concatenate([zero, u_ref[rws[0, 0, k + 1]]], axis=0).astype(BF16)
        a = blk[k : k + 2].reshape(256, 128)
        prod = jnp.dot(jnp.concatenate([u0, u1], axis=1), a, preferred_element_type=F32)
        acc_ref[jnp.where(k < count, cls[0, 0, k], spare)] += prod[:8]
        acc_ref[jnp.where(k + 1 < count, cls[0, 0, k + 1], spare)] += prod[8:]


def column(ref):
    rows = lax.broadcasted_iota(jnp.int32, (8, 128), 0)
    out = jnp.zeros((8, 128), F32)
    for s in range(8):
        out = jnp.where(rows == s, ref[s], out)
    return out


def lane_sum(x):
    return jnp.broadcast_to(jnp.sum(x, axis=1, keepdims=True), (8, 128))


def squares(ref, blocks):
    total = jnp.zeros((8, 128), F32)
    for b in range(blocks):
        total = total + ref[b] * ref[b]
    return lane_sum(total)


def store_pairs(acc_ref, out_ref, blocks):
    for b in range(0, blocks, 2):
        pair = jnp.concatenate([acc_ref[b], acc_ref[b + 1]], axis=0)
        out_ref[b // 2] = pair.astype(BF16)


def place_halves(own, other, out_ref):
    half = own.shape[1] // 128
    row = lax.axis_index("row")
    for b in range(half):
        out_ref[row * half + b] = own[:, b * 128 : (b + 1) * 128]
        out_ref[(1 - row) * half + b] = other[:, b * 128 : (b + 1) * 128]


def first_forward(
    alpha_hbm, rws_hbm, cls_hbm, cnt_hbm, blk_hbm, own_hbm, other_hbm, u_hbm,
    out, v_out, blk,
    alpha, rws, cls, cnt, own, other, u_piece, acc, small_sems, sems,
):
    small = [
        pltpu.make_async_copy(src, dst, small_sems.at[i])
        for i, (src, dst) in enumerate(
            (
                (rws_hbm, rws),
                (cls_hbm, cls),
                (cnt_hbm, cnt),
                (own_hbm, own),
                (other_hbm, other),
                (alpha_hbm, alpha),
                (u_hbm, u_piece),
            )
        )
    ]
    chunk = blk.shape[0] // sems.shape[0]
    large = [
        pltpu.make_async_copy(
            blk_hbm.at[0, 0, pl.ds(i * chunk, chunk)], blk.at[pl.ds(i * chunk, chunk)], sems.at[i]
        )
        for i in range(sems.shape[0])
    ]
    for copy in small + large:
        copy.start()
    for copy in small:
        copy.wait()
    place_halves(own, other, v_out)

    def ready(k):
        if k % chunk == 0:
            large[k // chunk].wait()

    forward(blk, rws, cls, cnt, v_out, acc, ready)
    pieces = u_piece.shape[1] // 128
    base = lax.axis_index("col") * pieces
    a = column(alpha)
    for b in range(pieces):
        acc[base + b] -= a * u_piece[:, b * 128 : (b + 1) * 128]
    store_pairs(acc, out, acc.shape[0] - 1)


def first_backward(rws, cls, cnt, blk, sum0, sum1, upd, message, acc):
    blocks = upd.shape[0]
    for b in range(blocks // 2):
        s = sum0[b].astype(F32) + sum1[b].astype(F32)
        upd[2 * b] = s[:8]
        upd[2 * b + 1] = s[8:]
    backward(blk, rws, cls, cnt, upd, acc)
    cells = acc.shape[0] - 1
    message[:cells] = acc[:cells]
    message[cells] = squares(upd, blocks)


def next_forward(total_rays, rws, cls, cnt, blk, own, other, v_old, out, vupd, beta_out, acc):
    cells = v_old.shape[0]
    beta = jnp.sqrt((own[cells] + other[cells]) / total_rays + EPS)
    beta_out[...] = beta
    inv = 1.0 / beta
    for b in range(cells):
        vupd[b] = (own[b] + other[b]) * inv - beta * v_old[b]
    forward(blk, rws, cls, cnt, vupd, acc)
    rays = acc.shape[0] - 1
    store_pairs(acc, out, rays)
    sq = squares(vupd, cells)
    lanes = lax.broadcasted_iota(jnp.int32, (8, 128), 1)
    sq = jnp.where(lanes == lax.axis_index("col"), sq, 0.0)
    high = sq.astype(BF16).astype(F32)
    out[rays // 2] = jnp.concatenate([high, sq - high], axis=0).astype(BF16)


def next_backward(
    total_cells, pieces, rws, cls, cnt, blk, sum0, sum1, old, beta, message, u_piece, alpha_out, upd, acc
):
    blocks = upd.shape[0]
    tail = sum0[blocks // 2].astype(F32) + sum1[blocks // 2].astype(F32)
    alpha = jnp.sqrt(lane_sum(tail[:8] + tail[8:]) / total_cells + EPS)
    alpha_out[...] = alpha
    inv = 1.0 / alpha
    ratio = alpha / beta[...]
    for b in range(blocks // 2):
        s = sum0[b].astype(F32) + sum1[b].astype(F32)
        upd[2 * b] = s[:8] * inv - ratio * old[2 * b]
        upd[2 * b + 1] = s[8:] * inv - ratio * old[2 * b + 1]
    backward(blk, rws, cls, cnt, upd, acc)
    cells = acc.shape[0] - 1
    message[:cells] = acc[:cells]
    message[cells] = squares(upd, blocks)
    base = lax.axis_index("col") * pieces
    for b in range(pieces):
        u_piece[b] = upd[base + b]


def last_cells(total_rays, own, other, v_old, alpha, sq, vupd, beta_out):
    cells = v_old.shape[0]
    beta = jnp.sqrt((own[cells] + other[cells]) / total_rays + EPS)
    beta_out[...] = beta
    inv = 1.0 / beta
    scale = beta / alpha[...]
    for b in range(cells):
        vupd[b] = (own[b] + other[b]) * inv - scale * v_old[b]
    sq[...] = squares(vupd, cells)


def finish(
    total_cells,
    phibar_in,
    rhobar_in,
    sq,
    sq_other,
    v1,
    v2,
    u_piece,
    x_in,
    w_in,
    beta1,
    alpha1,
    beta2,
    u_out,
    v_out,
    x_out,
    w_out,
    scalars,
):
    total = jnp.where(lax.axis_index("row") == 1, sq[...], sq_other[...])
    alpha2 = jnp.sqrt(total / total_cells + EPS)
    phibar, rhobar = column(phibar_in), column(rhobar_in)
    steps = []
    for beta, alpha in ((beta1[...], alpha1[...]), (beta2[...], alpha2)):
        rho = jnp.sqrt(rhobar * rhobar + beta * beta)
        cosine, sine = rhobar / rho, beta / rho
        steps.append((cosine * phibar / rho, sine * alpha / rho, 1.0 / alpha))
        rhobar = -cosine * alpha
        phibar = sine * phibar
    half = x_in.shape[1] // 128
    base = lax.axis_index("row") * half
    for b in range(half):
        at = slice(b * 128, (b + 1) * 128)
        x, w = x_in[:, at], w_in[:, at]
        for (along, back, inv), vupd in zip(steps, (v1, v2)):
            v = vupd[base + b] * inv
            x = x + along * w
            w = v - back * w
        v_out[:, at], x_out[:, at], w_out[:, at] = v, x, w
    inv = 1.0 / beta2[...]
    for b in range(u_piece.shape[0]):
        u_out[:, b * 128 : (b + 1) * 128] = u_piece[b] * inv
    rows = lax.broadcasted_iota(jnp.int32, (8, 128), 0)
    lanes = lax.broadcasted_iota(jnp.int32, (8, 128), 1)
    for i, value in enumerate((alpha2, phibar, rhobar)):
        line = jnp.sum(jnp.where(rows == lanes, value, 0.0), axis=0, keepdims=True)
        scalars[i : i + 1, :] = line[:, :8]


def other_core(x):
    return lax.ppermute(x, "row", [(0, 1), (1, 0)])


def column_sum(x):
    n = lax.axis_size("col")
    m = 1
    while True:
        y = lax.ppermute(x, "col", [(i, i ^ m) for i in range(n)])
        m *= 2
        if m >= n:
            return x, y
        x = (x.astype(F32) + y.astype(F32)).astype(BF16)


def last_sum(x):
    n = lax.axis_size("col")
    m = 1
    while m < n:
        x = x + lax.ppermute(x, ("row", "col"), [(n + i, n + (i ^ m)) for i in range(n)])
        m *= 2
    return x, lax.ppermute(x, "row", [(1, 0)])


def body(
    blocks, block_rows, block_cols, counts, u_rays, v_cells, x_cells, w_cells, alpha, phibar, rhobar
):
    n_row = lax.axis_size("row")
    n_col = lax.axis_size("col")
    pieces = u_rays.shape[1] // 128
    half = v_cells.shape[1] // 128
    rays = pieces * n_col
    cells = half * n_row
    total_rays = float(rays * 128 * n_row)
    total_cells = float(cells * 128 * n_col)
    where = (block_rows, block_cols, counts)
    listed = [SMEM] * 3
    ray_acc = pltpu.VMEM((rays + 1, 8, 128), F32)
    cell_acc = pltpu.VMEM((cells + 1, 8, 128), F32)

    slots = blocks.shape[2]
    part, v0, blk = call(
        first_forward,
        (
            shape(rays // 2, 16, 128, dtype=BF16),
            shape(cells, 8, 128),
            shape(slots, 128, 128, dtype=BF16),
        ),
        [HBM] * 8,
        [
            pltpu.SMEM(alpha.shape, F32),
            pltpu.SMEM(block_rows.shape, jnp.int32),
            pltpu.SMEM(block_cols.shape, jnp.int32),
            pltpu.SMEM(counts.shape, jnp.int32),
            pltpu.VMEM(v_cells.shape, F32),
            pltpu.VMEM(v_cells.shape, F32),
            pltpu.VMEM(u_rays.shape, F32),
            ray_acc,
            pltpu.SemaphoreType.DMA((7,)),
            pltpu.SemaphoreType.DMA((8,)),
        ],
    )(alpha, *where, blocks, v_cells, other_core(v_cells), u_rays)
    sum0, sum1 = column_sum(part)
    upd1, message = call(
        first_backward,
        (shape(rays, 8, 128), shape(cells + 1, 8, 128)),
        listed + [VMEM] * 3,
        [cell_acc],
    )(*where, blk, sum0, sum1)
    part, v1, beta1 = call(
        functools.partial(next_forward, total_rays),
        (shape(rays // 2 + 1, 16, 128, dtype=BF16), shape(cells, 8, 128), shape(8, 128)),
        listed + [VMEM] * 4,
        [ray_acc],
    )(*where, blk, message, other_core(message), v0)
    sum0, sum1 = column_sum(part)
    message, u_piece, alpha1 = call(
        functools.partial(next_backward, total_cells, pieces),
        (shape(cells + 1, 8, 128), shape(pieces, 8, 128), shape(8, 128)),
        listed + [VMEM] * 5,
        [pltpu.VMEM((rays, 8, 128), F32), cell_acc],
    )(*where, blk, sum0, sum1, upd1, beta1)
    sq, v2, beta2 = call(
        functools.partial(last_cells, total_rays),
        (shape(8, 128), shape(cells, 8, 128), shape(8, 128)),
        [VMEM] * 4,
    )(message, other_core(message), v1, alpha1)
    sq, sq_other = last_sum(sq)
    flat = shape(*v_cells.shape)
    return call(
        functools.partial(finish, total_cells),
        (shape(*u_rays.shape), flat, flat, flat, shape(3, 8)),
        [SMEM] * 2 + [VMEM] * 10,
    )(phibar, rhobar, sq, sq_other, v1, v2, u_piece, x_cells, w_cells, beta1, alpha1, beta2)


def solution(mesh):
    placed = (
        P(("region", "row"), "col", None, None, None),
        P(("region", "row"), "col", None),
        P(("region", "row"), "col", None),
        P(("region", "row"), "col"),
        P(None, ("region", "row", "col")),
        P(None, ("region", "col", "row")),
        P(None, ("region", "col", "row")),
        P(None, ("region", "col", "row")),
        P("region"),
        P("region"),
        P("region"),
    )
    return jax.shard_map(
        body,
        mesh=mesh,
        in_specs=placed,
        out_specs=(
            P(None, ("region", "row", "col")),
            P(None, ("region", "col", "row")),
            P(None, ("region", "col", "row")),
            P(None, ("region", "col", "row")),
            P(None, "region"),
        ),
        check_vma=False,
    )
```

```python
import functools

import jax
import jax.numpy as jnp
from jax import lax
from jax.experimental import pallas as pl
from jax.experimental.pallas import tpu as pltpu
from jax.sharding import PartitionSpec as P

ITERS = 2
EPS = 1e-6
F32 = jnp.float32
BF16 = jnp.bfloat16
SMEM = pl.BlockSpec(memory_space=pltpu.SMEM)
HBM = pl.BlockSpec(memory_space=pltpu.HBM)
VMEM = pl.BlockSpec(memory_space=pltpu.VMEM)


def call(kernel, out_shape, in_specs, scratch=()):
    return pl.pallas_call(
        kernel,
        out_shape=out_shape,
        in_specs=in_specs,
        out_specs=jax.tree.map(lambda _: VMEM, out_shape),
        scratch_shapes=list(scratch),
        compiler_params=pltpu.CompilerParams(vmem_limit_bytes=48 * 1024 * 1024),
    )


def shape(*dims, dtype=F32):
    return jax.ShapeDtypeStruct(dims, dtype)


def forward(blk, rws, cls, cnt, v_ref, acc_ref, ready=None):
    spare = acc_ref.shape[0] - 1
    count = cnt[0]
    acc_ref[...] = jnp.zeros_like(acc_ref)
    for k in range(0, blk.shape[0], 2):
        if ready is not None:
            ready(k)
        pair = jnp.concatenate([v_ref[cls[0, 0, k]], v_ref[cls[0, 0, k + 1]]], axis=0)
        a = blk[k : k + 2].reshape(256, 128)
        prod = lax.dot_general(
            pair.astype(BF16), a, (((1,), (1,)), ((), ())), preferred_element_type=F32
        )
        acc_ref[jnp.where(k < count, rws[0, 0, k], spare)] += prod[:8, :128]
        acc_ref[jnp.where(k + 1 < count, rws[0, 0, k + 1], spare)] += prod[8:, 128:]


def backward(blk, rws, cls, cnt, u_ref, acc_ref):
    spare = acc_ref.shape[0] - 1
    count = cnt[0]
    acc_ref[...] = jnp.zeros_like(acc_ref)
    zero = jnp.zeros((8, 128), F32)
    for k in range(0, blk.shape[0], 2):
        u0 = jnp.concatenate([u_ref[rws[0, 0, k]], zero], axis=0).astype(BF16)
        u1 = jnp.concatenate([zero, u_ref[rws[0, 0, k + 1]]], axis=0).astype(BF16)
        a = blk[k : k + 2].reshape(256, 128)
        prod = jnp.dot(jnp.concatenate([u0, u1], axis=1), a, preferred_element_type=F32)
        acc_ref[jnp.where(k < count, cls[0, 0, k], spare)] += prod[:8]
        acc_ref[jnp.where(k + 1 < count, cls[0, 0, k + 1], spare)] += prod[8:]


def column(ref):
    rows = lax.broadcasted_iota(jnp.int32, (8, 128), 0)
    out = jnp.zeros((8, 128), F32)
    for s in range(8):
        out = jnp.where(rows == s, ref[s], out)
    return out


def lane_sum(x):
    return jnp.broadcast_to(jnp.sum(x, axis=1, keepdims=True), (8, 128))


def squares(ref, blocks):
    total = jnp.zeros((8, 128), F32)
    for b in range(blocks):
        total = total + ref[b] * ref[b]
    return lane_sum(total)


def store_pairs(acc_ref, out_ref, blocks):
    for b in range(0, blocks, 2):
        pair = jnp.concatenate([acc_ref[b], acc_ref[b + 1]], axis=0)
        out_ref[b // 2] = pair.astype(BF16)


def place_halves(own, other, out_ref):
    half = own.shape[1] // 128
    row = lax.axis_index("row")
    for b in range(half):
        out_ref[row * half + b] = own[:, b * 128 : (b + 1) * 128]
        out_ref[(1 - row) * half + b] = other[:, b * 128 : (b + 1) * 128]


def load(blk_hbm, blk, sem):
    copy = pltpu.make_async_copy(blk_hbm.at[0, 0], blk, sem)
    copy.start()
    copy.wait()


def first_forward(rws, cls, cnt, alpha, blk, own, other, u_piece, out, v_out, acc):
    place_halves(own, other, v_out)
    forward(blk, rws, cls, cnt, v_out, acc)
    pieces = u_piece.shape[1] // 128
    base = lax.axis_index("col") * pieces
    a = column(alpha)
    for b in range(pieces):
        acc[base + b] -= a * u_piece[:, b * 128 : (b + 1) * 128]
    store_pairs(acc, out, acc.shape[0] - 1)


def first_backward(rws, cls, cnt, blk, sum0, sum1, upd, message, acc):
    blocks = upd.shape[0]
    for b in range(blocks // 2):
        s = sum0[b].astype(F32) + sum1[b].astype(F32)
        upd[2 * b] = s[:8]
        upd[2 * b + 1] = s[8:]
    backward(blk, rws, cls, cnt, upd, acc)
    cells = acc.shape[0] - 1
    message[:cells] = acc[:cells]
    message[cells] = squares(upd, blocks)


def next_forward(total_rays, rws, cls, cnt, blk, own, other, v_old, out, vupd, beta_out, acc):
    cells = v_old.shape[0]
    beta = jnp.sqrt((own[cells] + other[cells]) / total_rays + EPS)
    beta_out[...] = beta
    inv = 1.0 / beta
    for b in range(cells):
        vupd[b] = (own[b] + other[b]) * inv - beta * v_old[b]
    forward(blk, rws, cls, cnt, vupd, acc)
    rays = acc.shape[0] - 1
    store_pairs(acc, out, rays)
    sq = squares(vupd, cells)
    lanes = lax.broadcasted_iota(jnp.int32, (8, 128), 1)
    sq = jnp.where(lanes == lax.axis_index("col"), sq, 0.0)
    high = sq.astype(BF16).astype(F32)
    out[rays // 2] = jnp.concatenate([high, sq - high], axis=0).astype(BF16)


def next_backward(
    total_cells, pieces, rws, cls, cnt, blk, sum0, sum1, old, beta, message, u_piece, alpha_out, upd, acc
):
    blocks = upd.shape[0]
    tail = sum0[blocks // 2].astype(F32) + sum1[blocks // 2].astype(F32)
    alpha = jnp.sqrt(lane_sum(tail[:8] + tail[8:]) / total_cells + EPS)
    alpha_out[...] = alpha
    inv = 1.0 / alpha
    ratio = alpha / beta[...]
    for b in range(blocks // 2):
        s = sum0[b].astype(F32) + sum1[b].astype(F32)
        upd[2 * b] = s[:8] * inv - ratio * old[2 * b]
        upd[2 * b + 1] = s[8:] * inv - ratio * old[2 * b + 1]
    backward(blk, rws, cls, cnt, upd, acc)
    cells = acc.shape[0] - 1
    message[:cells] = acc[:cells]
    message[cells] = squares(upd, blocks)
    base = lax.axis_index("col") * pieces
    for b in range(pieces):
        u_piece[b] = upd[base + b]


def last_cells(total_rays, own, other, v_old, alpha, sq, vupd, beta_out):
    cells = v_old.shape[0]
    beta = jnp.sqrt((own[cells] + other[cells]) / total_rays + EPS)
    beta_out[...] = beta
    inv = 1.0 / beta
    scale = beta / alpha[...]
    for b in range(cells):
        vupd[b] = (own[b] + other[b]) * inv - scale * v_old[b]
    sq[...] = squares(vupd, cells)


def finish(
    total_cells,
    phibar_in,
    rhobar_in,
    sq,
    v1,
    v2,
    u_piece,
    x_in,
    w_in,
    beta1,
    alpha1,
    beta2,
    u_out,
    v_out,
    x_out,
    w_out,
    scalars,
):
    alpha2 = jnp.sqrt(sq[...] / total_cells + EPS)
    phibar, rhobar = column(phibar_in), column(rhobar_in)
    steps = []
    for beta, alpha in ((beta1[...], alpha1[...]), (beta2[...], alpha2)):
        rho = jnp.sqrt(rhobar * rhobar + beta * beta)
        cosine, sine = rhobar / rho, beta / rho
        steps.append((cosine * phibar / rho, sine * alpha / rho, 1.0 / alpha))
        rhobar = -cosine * alpha
        phibar = sine * phibar
    half = x_in.shape[1] // 128
    base = lax.axis_index("row") * half
    for b in range(half):
        at = slice(b * 128, (b + 1) * 128)
        x, w = x_in[:, at], w_in[:, at]
        for (along, back, inv), vupd in zip(steps, (v1, v2)):
            v = vupd[base + b] * inv
            x = x + along * w
            w = v - back * w
        v_out[:, at], x_out[:, at], w_out[:, at] = v, x, w
    inv = 1.0 / beta2[...]
    for b in range(u_piece.shape[0]):
        u_out[:, b * 128 : (b + 1) * 128] = u_piece[b] * inv
    rows = lax.broadcasted_iota(jnp.int32, (8, 128), 0)
    lanes = lax.broadcasted_iota(jnp.int32, (8, 128), 1)
    for i, value in enumerate((alpha2, phibar, rhobar)):
        line = jnp.sum(jnp.where(rows == lanes, value, 0.0), axis=0, keepdims=True)
        scalars[i : i + 1, :] = line[:, :8]


def other_core(x):
    return lax.ppermute(x, "row", [(0, 1), (1, 0)])


def column_sum(x):
    n = lax.axis_size("col")
    m = 1
    while True:
        y = lax.ppermute(x, "col", [(i, i ^ m) for i in range(n)])
        m *= 2
        if m >= n:
            return x, y
        x = (x.astype(F32) + y.astype(F32)).astype(BF16)


def last_sum(x):
    n = lax.axis_size("col")
    m = 1
    while m < n:
        pairs = [(i + n * r, (i ^ m) + n * (1 - r)) for r in (0, 1) for i in range(n)]
        x = x + lax.ppermute(x, ("row", "col"), pairs)
        m *= 2
    return x


def body(
    blocks, block_rows, block_cols, counts, u_rays, v_cells, x_cells, w_cells, alpha, phibar, rhobar
):
    n_row = lax.axis_size("row")
    n_col = lax.axis_size("col")
    pieces = u_rays.shape[1] // 128
    half = v_cells.shape[1] // 128
    rays = pieces * n_col
    cells = half * n_row
    total_rays = float(rays * 128 * n_row)
    total_cells = float(cells * 128 * n_col)
    where = (block_rows, block_cols, counts.reshape(1))
    listed = [SMEM] * 3
    ray_acc = pltpu.VMEM((rays + 1, 8, 128), F32)
    cell_acc = pltpu.VMEM((cells + 1, 8, 128), F32)

    v_other = other_core(v_cells)
    blk = call(
        load,
        shape(*blocks.shape[2:], dtype=BF16),
        [HBM],
        [pltpu.SemaphoreType.DMA],
    )(blocks)
    part, v0 = call(
        first_forward,
        (shape(rays // 2, 16, 128, dtype=BF16), shape(cells, 8, 128)),
        listed + [SMEM] + [VMEM] * 4,
        [ray_acc],
    )(*where, alpha, blk, v_cells, v_other, u_rays)
    sum0, sum1 = column_sum(part)
    upd1, message = call(
        first_backward,
        (shape(rays, 8, 128), shape(cells + 1, 8, 128)),
        listed + [VMEM] * 3,
        [cell_acc],
    )(*where, blk, sum0, sum1)
    part, v1, beta1 = call(
        functools.partial(next_forward, total_rays),
        (shape(rays // 2 + 1, 16, 128, dtype=BF16), shape(cells, 8, 128), shape(8, 128)),
        listed + [VMEM] * 4,
        [ray_acc],
    )(*where, blk, message, other_core(message), v0)
    sum0, sum1 = column_sum(part)
    message, u_piece, alpha1 = call(
        functools.partial(next_backward, total_cells, pieces),
        (shape(cells + 1, 8, 128), shape(pieces, 8, 128), shape(8, 128)),
        listed + [VMEM] * 5,
        [pltpu.VMEM((rays, 8, 128), F32), cell_acc],
    )(*where, blk, sum0, sum1, upd1, beta1)
    sq, v2, beta2 = call(
        functools.partial(last_cells, total_rays),
        (shape(8, 128), shape(cells, 8, 128), shape(8, 128)),
        [VMEM] * 4,
    )(message, other_core(message), v1, alpha1)
    sq = last_sum(sq)
    flat = shape(*v_cells.shape)
    return call(
        functools.partial(finish, total_cells),
        (shape(*u_rays.shape), flat, flat, flat, shape(3, 8)),
        [SMEM] * 2 + [VMEM] * 9,
    )(phibar, rhobar, sq, v1, v2, u_piece, x_cells, w_cells, beta1, alpha1, beta2)


def solution(mesh):
    placed = (
        P(("region", "row"), "col", None, None, None),
        P(("region", "row"), "col", None),
        P(("region", "row"), "col", None),
        P(("region", "row"), "col"),
        P(None, ("region", "row", "col")),
        P(None, ("region", "col", "row")),
        P(None, ("region", "col", "row")),
        P(None, ("region", "col", "row")),
        P("region"),
        P("region"),
        P("region"),
    )
    return jax.shard_map(
        body,
        mesh=mesh,
        in_specs=placed,
        out_specs=(
            P(None, ("region", "row", "col")),
            P(None, ("region", "col", "row")),
            P(None, ("region", "col", "row")),
            P(None, ("region", "col", "row")),
            P(None, "region"),
        ),
        check_vma=False,
    )
```

```python
import functools

import jax
import jax.numpy as jnp
from jax import lax
from jax.experimental import pallas as pl
from jax.experimental.pallas import tpu as pltpu
from jax.sharding import PartitionSpec as P

ITERS = 2
EPS = 1e-6
F32 = jnp.float32
BF16 = jnp.bfloat16
SMEM = pl.BlockSpec(memory_space=pltpu.SMEM)
HBM = pl.BlockSpec(memory_space=pltpu.HBM)
VMEM = pl.BlockSpec(memory_space=pltpu.VMEM)


def call(kernel, out_shape, in_specs, scratch=()):
    return pl.pallas_call(
        kernel,
        out_shape=out_shape,
        in_specs=in_specs,
        out_specs=jax.tree.map(lambda _: VMEM, out_shape),
        scratch_shapes=list(scratch),
        compiler_params=pltpu.CompilerParams(vmem_limit_bytes=48 * 1024 * 1024),
    )


def shape(*dims, dtype=F32):
    return jax.ShapeDtypeStruct(dims, dtype)


def lists(rws_ref, cls_ref, rws, cls, sems):
    copies = [
        pltpu.make_async_copy(rws_ref, rws, sems.at[0]),
        pltpu.make_async_copy(cls_ref, cls, sems.at[1]),
    ]
    for copy in copies:
        copy.start()
    return copies


def used(count, k, prod):
    return jnp.where(count > k, prod, 0.0)


def forward(blks, rws, cls, cnt, v_ref, acc_ref, between=None):
    count = jnp.broadcast_to(cnt[...], (8, 128))
    acc_ref[...] = jnp.zeros_like(acc_ref)
    k = 0
    for blk in blks:
        if between is not None and k > 0:
            between()
        for at in range(0, blk.shape[0], 2):
            pair = jnp.concatenate([v_ref[cls[0, 0, k]], v_ref[cls[0, 0, k + 1]]], axis=0)
            a = blk[at : at + 2].reshape(256, 128)
            prod = lax.dot_general(
                pair.astype(BF16), a, (((1,), (1,)), ((), ())), preferred_element_type=F32
            )
            acc_ref[rws[0, 0, k]] += used(count, k, prod[:8, :128])
            acc_ref[rws[0, 0, k + 1]] += used(count, k + 1, prod[8:, 128:])
            k += 2


def backward(blks, rws, cls, cnt, u_ref, acc_ref):
    count = jnp.broadcast_to(cnt[...], (8, 128))
    acc_ref[...] = jnp.zeros_like(acc_ref)
    zero = jnp.zeros((8, 128), F32)
    k = 0
    for blk in blks:
        for at in range(0, blk.shape[0], 2):
            u0 = jnp.concatenate([u_ref[rws[0, 0, k]], zero], axis=0).astype(BF16)
            u1 = jnp.concatenate([zero, u_ref[rws[0, 0, k + 1]]], axis=0).astype(BF16)
            a = blk[at : at + 2].reshape(256, 128)
            prod = jnp.dot(jnp.concatenate([u0, u1], axis=1), a, preferred_element_type=F32)
            acc_ref[cls[0, 0, k]] += used(count, k, prod[:8])
            acc_ref[cls[0, 0, k + 1]] += used(count, k + 1, prod[8:])
            k += 2


def column(ref):
    rows = lax.broadcasted_iota(jnp.int32, (8, 128), 0)
    out = jnp.zeros((8, 128), F32)
    for s in range(8):
        out = jnp.where(rows == s, ref[s], out)
    return out


def lane_sum(x):
    return jnp.broadcast_to(jnp.sum(x, axis=1, keepdims=True), (8, 128))


def squares(ref, blocks):
    total = jnp.zeros((8, 128), F32)
    for b in range(blocks):
        total = total + ref[b] * ref[b]
    return lane_sum(total)


def store_pairs(acc_ref, out_ref, blocks):
    for b in range(0, blocks, 2):
        pair = jnp.concatenate([acc_ref[b], acc_ref[b + 1]], axis=0)
        out_ref[b // 2] = pair.astype(BF16)


def place_halves(own, other, out_ref):
    half = own.shape[1] // 128
    row = lax.axis_index("row")
    for b in range(half):
        out_ref[row * half + b] = own[:, b * 128 : (b + 1) * 128]
        out_ref[(1 - row) * half + b] = other[:, b * 128 : (b + 1) * 128]


def load(blk_hbm, blk, sem):
    copy = pltpu.make_async_copy(blk_hbm.at[0, 0, pl.ds(0, blk.shape[0])], blk, sem)
    copy.start()
    copy.wait()


def first_forward(
    rws_ref, cls_ref, cnt, alpha, blk0, blk_hbm, own, other, u_piece,
    out, v_out, blk1,
    rws, cls, sems, sem, acc,
):
    rest = blk1.shape[0]
    copy = pltpu.make_async_copy(blk_hbm.at[0, 0, pl.ds(blk0.shape[0], rest)], blk1, sem)
    copy.start()
    copies = lists(rws_ref, cls_ref, rws, cls, sems)
    place_halves(own, other, v_out)
    for c in copies:
        c.wait()
    forward((blk0, blk1), rws, cls, cnt, v_out, acc, copy.wait)
    pieces = u_piece.shape[1] // 128
    base = lax.axis_index("col") * pieces
    a = column(alpha)
    for b in range(pieces):
        acc[base + b] -= a * u_piece[:, b * 128 : (b + 1) * 128]
    store_pairs(acc, out, acc.shape[0])


def first_backward(rws_ref, cls_ref, cnt, blk0, blk1, sum0, sum1, upd, message, rws, cls, sems, acc):
    copies = lists(rws_ref, cls_ref, rws, cls, sems)
    blocks = upd.shape[0]
    for b in range(blocks // 2):
        s = sum0[b].astype(F32) + sum1[b].astype(F32)
        upd[2 * b] = s[:8]
        upd[2 * b + 1] = s[8:]
    cells = acc.shape[0]
    message[cells] = squares(upd, blocks)
    for c in copies:
        c.wait()
    backward((blk0, blk1), rws, cls, cnt, upd, acc)
    message[:cells] = acc[...]


def next_forward(
    total_rays,
    rws_ref, cls_ref, cnt, blk0, blk1, own, other, v_old,
    out, vupd, beta_out,
    rws, cls, sems, acc,
):
    copies = lists(rws_ref, cls_ref, rws, cls, sems)
    cells = v_old.shape[0]
    beta = jnp.sqrt((own[cells] + other[cells]) / total_rays + EPS)
    beta_out[...] = beta
    inv = 1.0 / beta
    for b in range(cells):
        vupd[b] = (own[b] + other[b]) * inv - beta * v_old[b]
    rays = acc.shape[0]
    sq = squares(vupd, cells)
    lanes = lax.broadcasted_iota(jnp.int32, (8, 128), 1)
    sq = jnp.where(lanes == lax.axis_index("col"), sq, 0.0)
    high = sq.astype(BF16).astype(F32)
    out[rays // 2] = jnp.concatenate([high, sq - high], axis=0).astype(BF16)
    for c in copies:
        c.wait()
    forward((blk0, blk1), rws, cls, cnt, vupd, acc)
    store_pairs(acc, out, rays)


def next_backward(
    total_cells, pieces,
    rws_ref, cls_ref, cnt, blk0, blk1, sum0, sum1, old, beta,
    message, u_piece, alpha_out,
    rws, cls, sems, upd, acc,
):
    copies = lists(rws_ref, cls_ref, rws, cls, sems)
    blocks = upd.shape[0]
    tail = sum0[blocks // 2].astype(F32) + sum1[blocks // 2].astype(F32)
    alpha = jnp.sqrt(lane_sum(tail[:8] + tail[8:]) / total_cells + EPS)
    alpha_out[...] = alpha
    inv = 1.0 / alpha
    ratio = alpha / beta[...]
    for b in range(blocks // 2):
        s = sum0[b].astype(F32) + sum1[b].astype(F32)
        upd[2 * b] = s[:8] * inv - ratio * old[2 * b]
        upd[2 * b + 1] = s[8:] * inv - ratio * old[2 * b + 1]
    cells = acc.shape[0]
    message[cells] = squares(upd, blocks)
    base = lax.axis_index("col") * pieces
    for b in range(pieces):
        u_piece[b] = upd[base + b]
    for c in copies:
        c.wait()
    backward((blk0, blk1), rws, cls, cnt, upd, acc)
    message[:cells] = acc[...]


def last_cells(total_rays, own, other, v_old, alpha, sq, vupd, beta_out):
    cells = v_old.shape[0]
    beta = jnp.sqrt((own[cells] + other[cells]) / total_rays + EPS)
    beta_out[...] = beta
    inv = 1.0 / beta
    scale = beta / alpha[...]
    for b in range(cells):
        vupd[b] = (own[b] + other[b]) * inv - scale * v_old[b]
    sq[...] = squares(vupd, cells)


def finish(
    total_cells,
    phibar_in,
    rhobar_in,
    sq,
    v1,
    v2,
    u_piece,
    x_in,
    w_in,
    beta1,
    alpha1,
    beta2,
    u_out,
    v_out,
    x_out,
    w_out,
    scalars,
):
    alpha2 = jnp.sqrt(sq[...] / total_cells + EPS)
    phibar, rhobar = column(phibar_in), column(rhobar_in)
    steps = []
    for beta, alpha in ((beta1[...], alpha1[...]), (beta2[...], alpha2)):
        rho = jnp.sqrt(rhobar * rhobar + beta * beta)
        cosine, sine = rhobar / rho, beta / rho
        steps.append((cosine * phibar / rho, sine * alpha / rho, 1.0 / alpha))
        rhobar = -cosine * alpha
        phibar = sine * phibar
    half = x_in.shape[1] // 128
    base = lax.axis_index("row") * half
    for b in range(half):
        at = slice(b * 128, (b + 1) * 128)
        x, w = x_in[:, at], w_in[:, at]
        for (along, back, inv), vupd in zip(steps, (v1, v2)):
            v = vupd[base + b] * inv
            x = x + along * w
            w = v - back * w
        v_out[:, at], x_out[:, at], w_out[:, at] = v, x, w
    inv = 1.0 / beta2[...]
    for b in range(u_piece.shape[0]):
        u_out[:, b * 128 : (b + 1) * 128] = u_piece[b] * inv
    rows = lax.broadcasted_iota(jnp.int32, (8, 128), 0)
    lanes = lax.broadcasted_iota(jnp.int32, (8, 128), 1)
    for i, value in enumerate((alpha2, phibar, rhobar)):
        line = jnp.sum(jnp.where(rows == lanes, value, 0.0), axis=0, keepdims=True)
        scalars[i : i + 1, :] = line[:, :8]


def other_core(x):
    return lax.ppermute(x, "row", [(0, 1), (1, 0)])


def column_sum(x):
    n = lax.axis_size("col")
    m = 1
    while True:
        y = lax.ppermute(x, "col", [(i, i ^ m) for i in range(n)])
        m *= 2
        if m >= n:
            return x, y
        x = (x.astype(F32) + y.astype(F32)).astype(BF16)


def last_sum(x):
    n = lax.axis_size("col")
    m = 1
    while m < n:
        pairs = [(i + n * r, (i ^ m) + n * (1 - r)) for r in (0, 1) for i in range(n)]
        x = x + lax.ppermute(x, ("row", "col"), pairs)
        m *= 2
    return x


def body(
    blocks, block_rows, block_cols, counts, u_rays, v_cells, x_cells, w_cells, alpha, phibar, rhobar
):
    n_row = lax.axis_size("row")
    n_col = lax.axis_size("col")
    pieces = u_rays.shape[1] // 128
    half = v_cells.shape[1] // 128
    rays = pieces * n_col
    cells = half * n_row
    total_rays = float(rays * 128 * n_row)
    total_cells = float(cells * 128 * n_col)
    where = (block_rows, block_cols, counts)
    listed = [
        pltpu.SMEM(block_rows.shape, jnp.int32),
        pltpu.SMEM(block_cols.shape, jnp.int32),
        pltpu.SemaphoreType.DMA((2,)),
    ]
    ray_acc = pltpu.VMEM((rays, 8, 128), F32)
    cell_acc = pltpu.VMEM((cells, 8, 128), F32)
    slots = blocks.shape[2]
    half_blk = shape(slots // 2, 128, 128, dtype=BF16)

    v_other = other_core(v_cells)
    blk0 = call(load, half_blk, [HBM], [pltpu.SemaphoreType.DMA])(blocks)
    part, v0, blk1 = call(
        first_forward,
        (shape(rays // 2, 16, 128, dtype=BF16), shape(cells, 8, 128), half_blk),
        [VMEM] * 3 + [SMEM, VMEM, HBM] + [VMEM] * 3,
        listed + [pltpu.SemaphoreType.DMA, ray_acc],
    )(*where, alpha, blk0, blocks, v_cells, v_other, u_rays)
    operator = (*where, blk0, blk1)
    sum0, sum1 = column_sum(part)
    upd1, message = call(
        first_backward,
        (shape(rays, 8, 128), shape(cells + 1, 8, 128)),
        [VMEM] * 7,
        listed + [cell_acc],
    )(*operator, sum0, sum1)
    part, v1, beta1 = call(
        functools.partial(next_forward, total_rays),
        (shape(rays // 2 + 1, 16, 128, dtype=BF16), shape(cells, 8, 128), shape(8, 128)),
        [VMEM] * 8,
        listed + [ray_acc],
    )(*operator, message, other_core(message), v0)
    sum0, sum1 = column_sum(part)
    message, u_piece, alpha1 = call(
        functools.partial(next_backward, total_cells, pieces),
        (shape(cells + 1, 8, 128), shape(pieces, 8, 128), shape(8, 128)),
        [VMEM] * 9,
        listed + [pltpu.VMEM((rays, 8, 128), F32), cell_acc],
    )(*operator, sum0, sum1, upd1, beta1)
    sq, v2, beta2 = call(
        functools.partial(last_cells, total_rays),
        (shape(8, 128), shape(cells, 8, 128), shape(8, 128)),
        [VMEM] * 4,
    )(message, other_core(message), v1, alpha1)
    sq = last_sum(sq)
    flat = shape(*v_cells.shape)
    return call(
        functools.partial(finish, total_cells),
        (shape(*u_rays.shape), flat, flat, flat, shape(3, 8)),
        [SMEM] * 2 + [VMEM] * 9,
    )(phibar, rhobar, sq, v1, v2, u_piece, x_cells, w_cells, beta1, alpha1, beta2)


def solution(mesh):
    placed = (
        P(("region", "row"), "col", None, None, None),
        P(("region", "row"), "col", None),
        P(("region", "row"), "col", None),
        P(("region", "row"), "col"),
        P(None, ("region", "row", "col")),
        P(None, ("region", "col", "row")),
        P(None, ("region", "col", "row")),
        P(None, ("region", "col", "row")),
        P("region"),
        P("region"),
        P("region"),
    )
    return jax.shard_map(
        body,
        mesh=mesh,
        in_specs=placed,
        out_specs=(
            P(None, ("region", "row", "col")),
            P(None, ("region", "col", "row")),
            P(None, ("region", "col", "row")),
            P(None, ("region", "col", "row")),
            P(None, "region"),
        ),
        check_vma=False,
    )
```

```python
import functools

import jax
import jax.numpy as jnp
from jax import lax
from jax.experimental import pallas as pl
from jax.experimental.pallas import tpu as pltpu
from jax.sharding import PartitionSpec as P

ITERS = 2
EPS = 1e-6
F32 = jnp.float32
BF16 = jnp.bfloat16
SMEM = pl.BlockSpec(memory_space=pltpu.SMEM)
HBM = pl.BlockSpec(memory_space=pltpu.HBM)
VMEM = pl.BlockSpec(memory_space=pltpu.VMEM)


def call(kernel, out_shape, in_specs, scratch=(), cost=None):
    return pl.pallas_call(
        kernel,
        out_shape=out_shape,
        in_specs=in_specs,
        out_specs=jax.tree.map(lambda _: VMEM, out_shape),
        scratch_shapes=list(scratch),
        cost_estimate=cost,
        compiler_params=pltpu.CompilerParams(vmem_limit_bytes=48 * 1024 * 1024),
    )


def shape(*dims, dtype=F32):
    return jax.ShapeDtypeStruct(dims, dtype)


def lists(rws_ref, cls_ref, rws, cls, sems):
    copies = [
        pltpu.make_async_copy(rws_ref, rws, sems.at[0]),
        pltpu.make_async_copy(cls_ref, cls, sems.at[1]),
    ]
    for copy in copies:
        copy.start()
    return copies


def used(count, k, prod):
    return jnp.where(count > k, prod, 0.0)


def forward(blk, rws, cls, cnt, v_ref, acc_ref):
    count = jnp.broadcast_to(cnt[...], (8, 128))
    acc_ref[...] = jnp.zeros_like(acc_ref)
    for k in range(0, blk.shape[0], 2):
        pair = jnp.concatenate([v_ref[cls[0, 0, k]], v_ref[cls[0, 0, k + 1]]], axis=0)
        a = blk[k : k + 2].reshape(256, 128)
        prod = lax.dot_general(
            pair.astype(BF16), a, (((1,), (1,)), ((), ())), preferred_element_type=F32
        )
        acc_ref[rws[0, 0, k]] += used(count, k, prod[:8, :128])
        acc_ref[rws[0, 0, k + 1]] += used(count, k + 1, prod[8:, 128:])


def backward(blk, rws, cls, cnt, u_ref, acc_ref):
    count = jnp.broadcast_to(cnt[...], (8, 128))
    acc_ref[...] = jnp.zeros_like(acc_ref)
    zero = jnp.zeros((8, 128), F32)
    for k in range(0, blk.shape[0], 2):
        u0 = jnp.concatenate([u_ref[rws[0, 0, k]], zero], axis=0).astype(BF16)
        u1 = jnp.concatenate([zero, u_ref[rws[0, 0, k + 1]]], axis=0).astype(BF16)
        a = blk[k : k + 2].reshape(256, 128)
        prod = jnp.dot(jnp.concatenate([u0, u1], axis=1), a, preferred_element_type=F32)
        acc_ref[cls[0, 0, k]] += used(count, k, prod[:8])
        acc_ref[cls[0, 0, k + 1]] += used(count, k + 1, prod[8:])


def column(ref):
    rows = lax.broadcasted_iota(jnp.int32, (8, 128), 0)
    out = jnp.zeros((8, 128), F32)
    for s in range(8):
        out = jnp.where(rows == s, ref[s], out)
    return out


def lane_sum(x):
    return jnp.broadcast_to(jnp.sum(x, axis=1, keepdims=True), (8, 128))


def squares(ref, blocks):
    total = jnp.zeros((8, 128), F32)
    for b in range(blocks):
        total = total + ref[b] * ref[b]
    return lane_sum(total)


def store_pairs(acc_ref, out_ref, blocks):
    for b in range(0, blocks, 2):
        pair = jnp.concatenate([acc_ref[b], acc_ref[b + 1]], axis=0)
        out_ref[b // 2] = pair.astype(BF16)


def place_halves(own, other, out_ref):
    half = own.shape[1] // 128
    row = lax.axis_index("row")
    for b in range(half):
        out_ref[row * half + b] = own[:, b * 128 : (b + 1) * 128]
        out_ref[(1 - row) * half + b] = other[:, b * 128 : (b + 1) * 128]


def load(own_hbm, own, sem):
    copy = pltpu.make_async_copy(own_hbm, own, sem)
    copy.start()
    copy.wait()


def first_forward(
    rws_ref, cls_ref, cnt, alpha, blk, own, other, u_piece,
    out, v_out,
    rws, cls, sems, acc,
):
    copies = lists(rws_ref, cls_ref, rws, cls, sems)
    place_halves(own, other, v_out)
    for c in copies:
        c.wait()
    forward(blk, rws, cls, cnt, v_out, acc)
    pieces = u_piece.shape[1] // 128
    base = lax.axis_index("col") * pieces
    a = column(alpha)
    for b in range(pieces):
        acc[base + b] -= a * u_piece[:, b * 128 : (b + 1) * 128]
    store_pairs(acc, out, acc.shape[0])


def first_backward(rws_ref, cls_ref, cnt, blk, sum0, sum1, upd, message, rws, cls, sems, acc):
    copies = lists(rws_ref, cls_ref, rws, cls, sems)
    blocks = upd.shape[0]
    for b in range(blocks // 2):
        s = sum0[b].astype(F32) + sum1[b].astype(F32)
        upd[2 * b] = s[:8]
        upd[2 * b + 1] = s[8:]
    cells = acc.shape[0]
    message[cells] = squares(upd, blocks)
    for c in copies:
        c.wait()
    backward(blk, rws, cls, cnt, upd, acc)
    message[:cells] = acc[...]


def next_forward(
    total_rays,
    rws_ref, cls_ref, cnt, blk, own, other, v_old,
    out, vupd, beta_out,
    rws, cls, sems, acc,
):
    copies = lists(rws_ref, cls_ref, rws, cls, sems)
    cells = v_old.shape[0]
    beta = jnp.sqrt((own[cells] + other[cells]) / total_rays + EPS)
    beta_out[...] = beta
    inv = 1.0 / beta
    for b in range(cells):
        vupd[b] = (own[b] + other[b]) * inv - beta * v_old[b]
    rays = acc.shape[0]
    sq = squares(vupd, cells)
    lanes = lax.broadcasted_iota(jnp.int32, (8, 128), 1)
    sq = jnp.where(lanes == lax.axis_index("col"), sq, 0.0)
    high = sq.astype(BF16).astype(F32)
    out[rays // 2] = jnp.concatenate([high, sq - high], axis=0).astype(BF16)
    for c in copies:
        c.wait()
    forward(blk, rws, cls, cnt, vupd, acc)
    store_pairs(acc, out, rays)


def next_backward(
    total_cells, pieces,
    rws_ref, cls_ref, cnt, blk, sum0, sum1, old, beta,
    message, u_piece, alpha_out,
    rws, cls, sems, upd, acc,
):
    copies = lists(rws_ref, cls_ref, rws, cls, sems)
    blocks = upd.shape[0]
    tail = sum0[blocks // 2].astype(F32) + sum1[blocks // 2].astype(F32)
    alpha = jnp.sqrt(lane_sum(tail[:8] + tail[8:]) / total_cells + EPS)
    alpha_out[...] = alpha
    inv = 1.0 / alpha
    ratio = alpha / beta[...]
    for b in range(blocks // 2):
        s = sum0[b].astype(F32) + sum1[b].astype(F32)
        upd[2 * b] = s[:8] * inv - ratio * old[2 * b]
        upd[2 * b + 1] = s[8:] * inv - ratio * old[2 * b + 1]
    cells = acc.shape[0]
    message[cells] = squares(upd, blocks)
    base = lax.axis_index("col") * pieces
    for b in range(pieces):
        u_piece[b] = upd[base + b]
    for c in copies:
        c.wait()
    backward(blk, rws, cls, cnt, upd, acc)
    message[:cells] = acc[...]


def last_cells(total_rays, own, other, v_old, alpha, sq, vupd, beta_out):
    cells = v_old.shape[0]
    beta = jnp.sqrt((own[cells] + other[cells]) / total_rays + EPS)
    beta_out[...] = beta
    inv = 1.0 / beta
    scale = beta / alpha[...]
    for b in range(cells):
        vupd[b] = (own[b] + other[b]) * inv - scale * v_old[b]
    sq[...] = squares(vupd, cells)


def finish(
    total_cells,
    phibar_in,
    rhobar_in,
    sq,
    v1,
    v2,
    u_piece,
    x_in,
    w_in,
    beta1,
    alpha1,
    beta2,
    u_out,
    v_out,
    x_out,
    w_out,
    scalars,
):
    alpha2 = jnp.sqrt(sq[...] / total_cells + EPS)
    phibar, rhobar = column(phibar_in), column(rhobar_in)
    steps = []
    for beta, alpha in ((beta1[...], alpha1[...]), (beta2[...], alpha2)):
        rho = jnp.sqrt(rhobar * rhobar + beta * beta)
        cosine, sine = rhobar / rho, beta / rho
        steps.append((cosine * phibar / rho, sine * alpha / rho, 1.0 / alpha))
        rhobar = -cosine * alpha
        phibar = sine * phibar
    half = x_in.shape[1] // 128
    base = lax.axis_index("row") * half
    for b in range(half):
        at = slice(b * 128, (b + 1) * 128)
        x, w = x_in[:, at], w_in[:, at]
        for (along, back, inv), vupd in zip(steps, (v1, v2)):
            v = vupd[base + b] * inv
            x = x + along * w
            w = v - back * w
        v_out[:, at], x_out[:, at], w_out[:, at] = v, x, w
    inv = 1.0 / beta2[...]
    for b in range(u_piece.shape[0]):
        u_out[:, b * 128 : (b + 1) * 128] = u_piece[b] * inv
    rows = lax.broadcasted_iota(jnp.int32, (8, 128), 0)
    lanes = lax.broadcasted_iota(jnp.int32, (8, 128), 1)
    for i, value in enumerate((alpha2, phibar, rhobar)):
        line = jnp.sum(jnp.where(rows == lanes, value, 0.0), axis=0, keepdims=True)
        scalars[i : i + 1, :] = line[:, :8]


def other_core(x):
    return lax.ppermute(x, "row", [(0, 1), (1, 0)])


def column_sum(x):
    n = lax.axis_size("col")
    steps = [1 << i for i in range((n - 1).bit_length())]
    for first, second in zip(steps, steps[-1:] + steps[:-1]):
        pairs = [(i, i ^ first) for i in range(n)] + [(n + i, n + (i ^ second)) for i in range(n)]
        y = lax.ppermute(x, ("row", "col"), pairs)
        if first == steps[-1]:
            return x, y
        x = (x.astype(F32) + y.astype(F32)).astype(BF16)


def last_sum(x):
    n = lax.axis_size("col")
    m = 1
    while m < n:
        pairs = [(i + n * r, (i ^ m) + n * (1 - r)) for r in (0, 1) for i in range(n)]
        x = x + lax.ppermute(x, ("row", "col"), pairs)
        m *= 2
    return x


def body(
    blocks, block_rows, block_cols, counts, u_rays, v_cells, x_cells, w_cells, alpha, phibar, rhobar
):
    n_row = lax.axis_size("row")
    n_col = lax.axis_size("col")
    pieces = u_rays.shape[1] // 128
    half = v_cells.shape[1] // 128
    rays = pieces * n_col
    cells = half * n_row
    total_rays = float(rays * 128 * n_row)
    total_cells = float(cells * 128 * n_col)
    where = (block_rows, block_cols, counts)
    listed = [
        pltpu.SMEM(block_rows.shape, jnp.int32),
        pltpu.SMEM(block_cols.shape, jnp.int32),
        pltpu.SemaphoreType.DMA((2,)),
    ]
    ray_acc = pltpu.VMEM((rays, 8, 128), F32)
    cell_acc = pltpu.VMEM((cells, 8, 128), F32)
    own = call(
        load,
        shape(*v_cells.shape),
        [HBM],
        [pltpu.SemaphoreType.DMA],
        pl.CostEstimate(flops=5 * 10**9, bytes_accessed=1, transcendentals=0),
    )(v_cells)
    v_other = other_core(own)
    blk = blocks.reshape(blocks.shape[2:])
    part, v0 = call(
        first_forward,
        (shape(rays // 2, 16, 128, dtype=BF16), shape(cells, 8, 128)),
        [VMEM] * 3 + [SMEM] + [VMEM] * 4,
        listed + [ray_acc],
    )(*where, alpha, blk, own, v_other, u_rays)
    operator = (*where, blk)
    sum0, sum1 = column_sum(part)
    upd1, message = call(
        first_backward,
        (shape(rays, 8, 128), shape(cells + 1, 8, 128)),
        [VMEM] * 6,
        listed + [cell_acc],
    )(*operator, sum0, sum1)
    part, v1, beta1 = call(
        functools.partial(next_forward, total_rays),
        (shape(rays // 2 + 1, 16, 128, dtype=BF16), shape(cells, 8, 128), shape(8, 128)),
        [VMEM] * 7,
        listed + [ray_acc],
    )(*operator, message, other_core(message), v0)
    sum0, sum1 = column_sum(part)
    message, u_piece, alpha1 = call(
        functools.partial(next_backward, total_cells, pieces),
        (shape(cells + 1, 8, 128), shape(pieces, 8, 128), shape(8, 128)),
        [VMEM] * 8,
        listed + [pltpu.VMEM((rays, 8, 128), F32), cell_acc],
    )(*operator, sum0, sum1, upd1, beta1)
    sq, v2, beta2 = call(
        functools.partial(last_cells, total_rays),
        (shape(8, 128), shape(cells, 8, 128), shape(8, 128)),
        [VMEM] * 4,
    )(message, other_core(message), v1, alpha1)
    sq = last_sum(sq)
    flat = shape(*v_cells.shape)
    return call(
        functools.partial(finish, total_cells),
        (shape(*u_rays.shape), flat, flat, flat, shape(3, 8)),
        [SMEM] * 2 + [VMEM] * 9,
    )(phibar, rhobar, sq, v1, v2, u_piece, x_cells, w_cells, beta1, alpha1, beta2)


def solution(mesh):
    placed = (
        P(("region", "row"), "col", None, None, None),
        P(("region", "row"), "col", None),
        P(("region", "row"), "col", None),
        P(("region", "row"), "col"),
        P(None, ("region", "row", "col")),
        P(None, ("region", "col", "row")),
        P(None, ("region", "col", "row")),
        P(None, ("region", "col", "row")),
        P("region"),
        P("region"),
        P("region"),
    )
    return jax.shard_map(
        body,
        mesh=mesh,
        in_specs=placed,
        out_specs=(
            P(None, ("region", "row", "col")),
            P(None, ("region", "col", "row")),
            P(None, ("region", "col", "row")),
            P(None, ("region", "col", "row")),
            P(None, "region"),
        ),
        check_vma=False,
    )
```

```python
import functools

import jax
import jax.numpy as jnp
from jax import lax
from jax.experimental import pallas as pl
from jax.experimental.pallas import tpu as pltpu
from jax.sharding import PartitionSpec as P

ITERS = 2
EPS = 1e-6
F32 = jnp.float32
BF16 = jnp.bfloat16
SMEM = pl.BlockSpec(memory_space=pltpu.SMEM)
HBM = pl.BlockSpec(memory_space=pltpu.HBM)
VMEM = pl.BlockSpec(memory_space=pltpu.VMEM)


def call(kernel, out_shape, in_specs, scratch=(), cost=None):
    return pl.pallas_call(
        kernel,
        out_shape=out_shape,
        in_specs=in_specs,
        out_specs=jax.tree.map(lambda _: VMEM, out_shape),
        scratch_shapes=list(scratch),
        cost_estimate=cost,
        compiler_params=pltpu.CompilerParams(vmem_limit_bytes=48 * 1024 * 1024),
    )


def shape(*dims, dtype=F32):
    return jax.ShapeDtypeStruct(dims, dtype)


def lists(*pairs, sems):
    copies = [pltpu.make_async_copy(*pair, sems.at[i]) for i, pair in enumerate(pairs)]
    for copy in copies:
        copy.start()
    return copies


def used(count, k, prod):
    return jnp.where(count > k, prod, 0.0)


def forward(blk, rws, cls, cnt, v_ref, acc_ref):
    count = jnp.broadcast_to(cnt[...], (8, 128))
    acc_ref[...] = jnp.zeros_like(acc_ref)
    for k in range(0, blk.shape[0], 2):
        pair = jnp.concatenate([v_ref[cls[0, 0, k]], v_ref[cls[0, 0, k + 1]]], axis=0)
        a = blk[k : k + 2].reshape(256, 128)
        prod = lax.dot_general(
            pair.astype(BF16), a, (((1,), (1,)), ((), ())), preferred_element_type=F32
        )
        acc_ref[rws[0, 0, k]] += used(count, k, prod[:8, :128])
        acc_ref[rws[0, 0, k + 1]] += used(count, k + 1, prod[8:, 128:])


def backward(blk, rws, cls, cnt, u_ref, acc_ref):
    count = jnp.broadcast_to(cnt[...], (8, 128))
    acc_ref[...] = jnp.zeros_like(acc_ref)
    zero = jnp.zeros((8, 128), F32)
    for k in range(0, blk.shape[0], 2):
        u0 = jnp.concatenate([u_ref[rws[0, 0, k]], zero], axis=0).astype(BF16)
        u1 = jnp.concatenate([zero, u_ref[rws[0, 0, k + 1]]], axis=0).astype(BF16)
        a = blk[k : k + 2].reshape(256, 128)
        prod = jnp.dot(jnp.concatenate([u0, u1], axis=1), a, preferred_element_type=F32)
        acc_ref[cls[0, 0, k]] += used(count, k, prod[:8])
        acc_ref[cls[0, 0, k + 1]] += used(count, k + 1, prod[8:])


def column(ref):
    rows = lax.broadcasted_iota(jnp.int32, (8, 128), 0)
    out = jnp.zeros((8, 128), F32)
    for s in range(8):
        out = jnp.where(rows == s, ref[s], out)
    return out


def lane_sum(x):
    return jnp.broadcast_to(jnp.sum(x, axis=1, keepdims=True), (8, 128))


def squares(ref, blocks):
    total = jnp.zeros((8, 128), F32)
    for b in range(blocks):
        total = total + ref[b] * ref[b]
    return lane_sum(total)


def store_pairs(acc_ref, outs):
    half = acc_ref.shape[0] // 4
    for b in range(2 * half):
        pair = jnp.concatenate([acc_ref[2 * b], acc_ref[2 * b + 1]], axis=0)
        outs[b // half][b % half] = pair.astype(BF16)


def place_halves(own, other, out_ref):
    half = own.shape[1] // 128
    row = lax.axis_index("row")
    for b in range(half):
        out_ref[row * half + b] = own[:, b * 128 : (b + 1) * 128]
        out_ref[(1 - row) * half + b] = other[:, b * 128 : (b + 1) * 128]


def load(own_hbm, own, sem):
    copy = pltpu.make_async_copy(own_hbm, own, sem)
    copy.start()
    copy.wait()


def first_forward(
    rws_ref, cls_ref, cnt, blk, alpha_ref, own, other, u_piece,
    out0, out1, v_out,
    rws, cls, sems, alpha, acc,
):
    copies = lists((rws_ref, rws), (cls_ref, cls), (alpha_ref, alpha), sems=sems)
    place_halves(own, other, v_out)
    for c in copies:
        c.wait()
    forward(blk, rws, cls, cnt, v_out, acc)
    pieces = u_piece.shape[1] // 128
    base = lax.axis_index("col") * pieces
    a = column(alpha)
    for b in range(pieces):
        acc[base + b] -= a * u_piece[:, b * 128 : (b + 1) * 128]
    store_pairs(acc, (out0, out1))


def pair_sums(pairs, a0, a1, b0, b1):
    half = pairs // 2
    for b in range(pairs):
        one, two = (a0, a1) if b < half else (b0, b1)
        yield one[b % half].astype(F32) + two[b % half].astype(F32)


def first_backward(rws_ref, cls_ref, cnt, blk, sums0, sums1, sums2, sums3, upd, message, rws, cls, sems, acc):
    copies = lists((rws_ref, rws), (cls_ref, cls), sems=sems)
    blocks = upd.shape[0]
    for b, s in enumerate(pair_sums(blocks // 2, sums0, sums1, sums2, sums3)):
        upd[2 * b] = s[:8]
        upd[2 * b + 1] = s[8:]
    cells = acc.shape[0]
    message[cells] = squares(upd, blocks)
    for c in copies:
        c.wait()
    backward(blk, rws, cls, cnt, upd, acc)
    message[:cells] = acc[...]


def next_forward(
    total_rays,
    rws_ref, cls_ref, cnt, blk, own, other, v_old,
    out0, out1, vupd, beta_out,
    rws, cls, sems, acc,
):
    copies = lists((rws_ref, rws), (cls_ref, cls), sems=sems)
    cells = v_old.shape[0]
    beta = jnp.sqrt((own[cells] + other[cells]) / total_rays + EPS)
    beta_out[...] = beta
    inv = 1.0 / beta
    for b in range(cells):
        vupd[b] = (own[b] + other[b]) * inv - beta * v_old[b]
    rays = acc.shape[0]
    sq = squares(vupd, cells)
    lanes = lax.broadcasted_iota(jnp.int32, (8, 128), 1)
    sq = jnp.where(lanes == lax.axis_index("col"), sq, 0.0)
    high = sq.astype(BF16).astype(F32)
    out0[rays // 4] = jnp.concatenate([high, sq - high], axis=0).astype(BF16)
    for c in copies:
        c.wait()
    forward(blk, rws, cls, cnt, vupd, acc)
    store_pairs(acc, (out0, out1))


def next_backward(
    total_cells, pieces,
    rws_ref, cls_ref, cnt, blk, sums0, sums1, sums2, sums3, old, beta,
    message, u_piece, alpha_out,
    rws, cls, sems, upd, acc,
):
    copies = lists((rws_ref, rws), (cls_ref, cls), sems=sems)
    blocks = upd.shape[0]
    tail = sums0[blocks // 4].astype(F32) + sums1[blocks // 4].astype(F32)
    alpha = jnp.sqrt(lane_sum(tail[:8] + tail[8:]) / total_cells + EPS)
    alpha_out[...] = alpha
    inv = 1.0 / alpha
    ratio = alpha / beta[...]
    for b, s in enumerate(pair_sums(blocks // 2, sums0, sums1, sums2, sums3)):
        upd[2 * b] = s[:8] * inv - ratio * old[2 * b]
        upd[2 * b + 1] = s[8:] * inv - ratio * old[2 * b + 1]
    cells = acc.shape[0]
    message[cells] = squares(upd, blocks)
    base = lax.axis_index("col") * pieces
    for b in range(pieces):
        u_piece[b] = upd[base + b]
    for c in copies:
        c.wait()
    backward(blk, rws, cls, cnt, upd, acc)
    message[:cells] = acc[...]


def last_cells(total_rays, own, other, v_old, alpha, sq, vupd, beta_out):
    cells = v_old.shape[0]
    beta = jnp.sqrt((own[cells] + other[cells]) / total_rays + EPS)
    beta_out[...] = beta
    inv = 1.0 / beta
    scale = beta / alpha[...]
    for b in range(cells):
        vupd[b] = (own[b] + other[b]) * inv - scale * v_old[b]
    sq[...] = squares(vupd, cells)


def finish(
    total_cells,
    phibar_in,
    rhobar_in,
    sq,
    v1,
    v2,
    u_piece,
    x_in,
    w_in,
    beta1,
    alpha1,
    beta2,
    u_out,
    v_out,
    x_out,
    w_out,
    scalars,
):
    alpha2 = jnp.sqrt(sq[...] / total_cells + EPS)
    phibar, rhobar = column(phibar_in), column(rhobar_in)
    steps = []
    for beta, alpha in ((beta1[...], alpha1[...]), (beta2[...], alpha2)):
        rho = jnp.sqrt(rhobar * rhobar + beta * beta)
        cosine, sine = rhobar / rho, beta / rho
        steps.append((cosine * phibar / rho, sine * alpha / rho, 1.0 / alpha))
        rhobar = -cosine * alpha
        phibar = sine * phibar
    half = x_in.shape[1] // 128
    base = lax.axis_index("row") * half
    for b in range(half):
        at = slice(b * 128, (b + 1) * 128)
        x, w = x_in[:, at], w_in[:, at]
        for (along, back, inv), vupd in zip(steps, (v1, v2)):
            v = vupd[base + b] * inv
            x = x + along * w
            w = v - back * w
        v_out[:, at], x_out[:, at], w_out[:, at] = v, x, w
    inv = 1.0 / beta2[...]
    for b in range(u_piece.shape[0]):
        u_out[:, b * 128 : (b + 1) * 128] = u_piece[b] * inv
    rows = lax.broadcasted_iota(jnp.int32, (8, 128), 0)
    lanes = lax.broadcasted_iota(jnp.int32, (8, 128), 1)
    for i, value in enumerate((alpha2, phibar, rhobar)):
        line = jnp.sum(jnp.where(rows == lanes, value, 0.0), axis=0, keepdims=True)
        scalars[i : i + 1, :] = line[:, :8]


def other_core(x):
    return lax.ppermute(x, "row", [(0, 1), (1, 0)])


def column_sum(halves):
    n = lax.axis_size("col")
    steps = [1 << i for i in range((n - 1).bit_length())]
    turned = steps[-1:] + steps[:-1]
    orders = ((steps, turned), (steps, turned))
    xs = list(halves)
    for i in range(len(steps)):
        ys = [
            lax.ppermute(
                x,
                ("row", "col"),
                [(j, j ^ first[i]) for j in range(n)] + [(n + j, n + (j ^ second[i])) for j in range(n)],
            )
            for x, (first, second) in zip(xs, orders)
        ]
        if i == len(steps) - 1:
            return xs[0], ys[0], xs[1], ys[1]
        xs = [(x.astype(F32) + y.astype(F32)).astype(BF16) for x, y in zip(xs, ys)]


def last_sum(x):
    n = lax.axis_size("col")
    m = 1
    while m < n:
        pairs = [(i + n * r, (i ^ m) + n * (1 - r)) for r in (0, 1) for i in range(n)]
        x = x + lax.ppermute(x, ("row", "col"), pairs)
        m *= 2
    return x


def body(
    blocks, block_rows, block_cols, counts, u_rays, v_cells, x_cells, w_cells, alpha, phibar, rhobar
):
    n_row = lax.axis_size("row")
    n_col = lax.axis_size("col")
    pieces = u_rays.shape[1] // 128
    half = v_cells.shape[1] // 128
    rays = pieces * n_col
    cells = half * n_row
    total_rays = float(rays * 128 * n_row)
    total_cells = float(cells * 128 * n_col)
    where = (block_rows, block_cols, counts)
    listed = [
        pltpu.SMEM(block_rows.shape, jnp.int32),
        pltpu.SMEM(block_cols.shape, jnp.int32),
        pltpu.SemaphoreType.DMA((3,)),
    ]
    ray_acc = pltpu.VMEM((rays, 8, 128), F32)
    cell_acc = pltpu.VMEM((cells, 8, 128), F32)
    own = call(
        load,
        shape(*v_cells.shape),
        [HBM],
        [pltpu.SemaphoreType.DMA],
        pl.CostEstimate(flops=5 * 10**9, bytes_accessed=1, transcendentals=0),
    )(v_cells)
    v_other = other_core(own)
    blk = blocks.reshape(blocks.shape[2:])
    operator = (*where, blk)
    half_rays = shape(rays // 4, 16, 128, dtype=BF16)
    *part, v0 = call(
        first_forward,
        (half_rays, half_rays, shape(cells, 8, 128)),
        [VMEM] * 8,
        listed + [pltpu.SMEM(alpha.shape, F32), ray_acc],
    )(*operator, alpha, own, v_other, u_rays)
    sums = column_sum(part)
    upd1, message = call(
        first_backward,
        (shape(rays, 8, 128), shape(cells + 1, 8, 128)),
        [VMEM] * 8,
        listed + [cell_acc],
    )(*operator, *sums)
    *part, v1, beta1 = call(
        functools.partial(next_forward, total_rays),
        (shape(rays // 4 + 1, 16, 128, dtype=BF16), half_rays, shape(cells, 8, 128), shape(8, 128)),
        [VMEM] * 7,
        listed + [ray_acc],
    )(*operator, message, other_core(message), v0)
    sums = column_sum(part)
    message, u_piece, alpha1 = call(
        functools.partial(next_backward, total_cells, pieces),
        (shape(cells + 1, 8, 128), shape(pieces, 8, 128), shape(8, 128)),
        [VMEM] * 10,
        listed + [pltpu.VMEM((rays, 8, 128), F32), cell_acc],
    )(*operator, *sums, upd1, beta1)
    sq, v2, beta2 = call(
        functools.partial(last_cells, total_rays),
        (shape(8, 128), shape(cells, 8, 128), shape(8, 128)),
        [VMEM] * 4,
    )(message, other_core(message), v1, alpha1)
    sq = last_sum(sq)
    flat = shape(*v_cells.shape)
    return call(
        functools.partial(finish, total_cells),
        (shape(*u_rays.shape), flat, flat, flat, shape(3, 8)),
        [SMEM] * 2 + [VMEM] * 9,
    )(phibar, rhobar, sq, v1, v2, u_piece, x_cells, w_cells, beta1, alpha1, beta2)


def solution(mesh):
    placed = (
        P(("region", "row"), "col", None, None, None),
        P(("region", "row"), "col", None),
        P(("region", "row"), "col", None),
        P(("region", "row"), "col"),
        P(None, ("region", "row", "col")),
        P(None, ("region", "col", "row")),
        P(None, ("region", "col", "row")),
        P(None, ("region", "col", "row")),
        P("region"),
        P("region"),
        P("region"),
    )
    return jax.shard_map(
        body,
        mesh=mesh,
        in_specs=placed,
        out_specs=(
            P(None, ("region", "row", "col")),
            P(None, ("region", "col", "row")),
            P(None, ("region", "col", "row")),
            P(None, ("region", "col", "row")),
            P(None, "region"),
        ),
        check_vma=False,
    )
```

```python
import functools

import jax
import jax.numpy as jnp
from jax import lax
from jax.experimental import pallas as pl
from jax.experimental.pallas import tpu as pltpu
from jax.sharding import PartitionSpec as P

ITERS = 2
EPS = 1e-6
F32 = jnp.float32
BF16 = jnp.bfloat16
SMEM = pl.BlockSpec(memory_space=pltpu.SMEM)
HBM = pl.BlockSpec(memory_space=pltpu.HBM)
VMEM = pl.BlockSpec(memory_space=pltpu.VMEM)


def call(kernel, out_shape, in_specs, scratch=(), cost=None):
    return pl.pallas_call(
        kernel,
        out_shape=out_shape,
        in_specs=in_specs,
        out_specs=jax.tree.map(lambda _: VMEM, out_shape),
        scratch_shapes=list(scratch),
        cost_estimate=cost,
        compiler_params=pltpu.CompilerParams(vmem_limit_bytes=48 * 1024 * 1024),
    )


def shape(*dims, dtype=F32):
    return jax.ShapeDtypeStruct(dims, dtype)


def lists(*pairs, sems):
    copies = [pltpu.make_async_copy(*pair, sems.at[i]) for i, pair in enumerate(pairs)]
    for copy in copies:
        copy.start()
    return copies


def used(count, k, prod):
    return jnp.where(count > k, prod, 0.0)


def low_lanes():
    return lax.broadcasted_iota(jnp.int32, (8, 128), 1) < 64


def forward(part, blk, rws, cls, cnt, v_ref, acc_ref):
    low = low_lanes()
    count = jnp.broadcast_to(cnt[...], (8, 128))
    even, odd = jnp.where(low, count, 0), jnp.where(low, 0, count)
    acc_ref[...] = jnp.zeros_like(acc_ref)
    for k in range(0, blk.shape[0], 2):
        pair = jnp.concatenate([v_ref[cls[0, 0, k]], v_ref[cls[0, 0, k + 1]]], axis=0)
        a = blk[k : k + 2, 64 * part : 64 * part + 64].reshape(128, 128)
        prod = lax.dot_general(
            pair.astype(BF16), a, (((1,), (1,)), ((), ())), preferred_element_type=F32
        )
        acc_ref[rws[0, 0, k]] += used(even, k, prod[:8])
        acc_ref[rws[0, 0, k + 1]] += used(odd, k + 1, prod[8:])


def store_pairs(acc_ref, out):
    low = low_lanes()
    for t in range(acc_ref.shape[0] // 4):
        rows = []
        for r in (4 * t, 4 * t + 2):
            x, y = acc_ref[r], acc_ref[r + 1]
            rows.append(jnp.where(low, x + pltpu.roll(x, 64, 1), y + pltpu.roll(y, 64, 1)))
        out[t] = jnp.concatenate(rows, axis=0).astype(BF16)


def spread(upd, even, odd):
    low = low_lanes()
    for p in range(upd.shape[0]):
        x = upd[p]
        y = pltpu.roll(x, 64, 1)
        even[2 * p] = jnp.where(low, x, 0.0)
        even[2 * p + 1] = jnp.where(low, y, 0.0)
        odd[2 * p] = jnp.where(low, 0.0, y)
        odd[2 * p + 1] = jnp.where(low, 0.0, x)


def backward(part, blk, rws, cls, cnt, even, odd, acc_ref):
    count = jnp.broadcast_to(cnt[...], (8, 128))
    for k in range(0, blk.shape[0], 2):
        pair = jnp.concatenate([even[rws[0, 0, k]], odd[rws[0, 0, k + 1]]], axis=0)
        a = blk[k : k + 2, 64 * part : 64 * part + 64].reshape(128, 128)
        prod = jnp.dot(pair.astype(BF16), a, preferred_element_type=F32)
        acc_ref[cls[0, 0, k]] += used(count, k, prod[:8])
        acc_ref[cls[0, 0, k + 1]] += used(count, k + 1, prod[8:])


def column(ref):
    rows = lax.broadcasted_iota(jnp.int32, (8, 128), 0)
    out = jnp.zeros((8, 128), F32)
    for s in range(8):
        out = jnp.where(rows == s, ref[s], out)
    return out


def lane_sum(x):
    return jnp.broadcast_to(jnp.sum(x, axis=1, keepdims=True), (8, 128))


def squares(ref, blocks):
    totals = [jnp.zeros((8, 128), F32)] * 4
    for b in range(blocks):
        totals[b % 4] = totals[b % 4] + ref[b] * ref[b]
    return lane_sum((totals[0] + totals[1]) + (totals[2] + totals[3]))


def place_halves(own, other, out_ref):
    half = own.shape[1] // 128
    row = lax.axis_index("row")
    for b in range(half):
        out_ref[row * half + b] = own[:, b * 128 : (b + 1) * 128]
        out_ref[(1 - row) * half + b] = other[:, b * 128 : (b + 1) * 128]


def load(own_hbm, own, sem):
    copy = pltpu.make_async_copy(own_hbm, own, sem)
    copy.start()
    copy.wait()


def first_sums(part, acc, alpha_ref, u_piece):
    pieces = u_piece.shape[1] // 128
    base = lax.axis_index("col") * pieces
    a = column(alpha_ref)
    mine = low_lanes() if part == 0 else jnp.logical_not(low_lanes())
    for b in range(pieces):
        acc[base + b] -= jnp.where(mine, a * u_piece[:, b * 128 : (b + 1) * 128], 0.0)


def first_forward_0(
    rws_ref, cls_ref, cnt, blk, alpha_ref, u_piece, own, other,
    out, v_out,
    rws, cls, sems, alpha, acc,
):
    copies = lists((rws_ref, rws), (cls_ref, cls), (alpha_ref, alpha), sems=sems)
    place_halves(own, other, v_out)
    for c in copies:
        c.wait()
    forward(0, blk, rws, cls, cnt, v_out, acc)
    first_sums(0, acc, alpha, u_piece)
    store_pairs(acc, out)


def first_forward_1(
    rws_ref, cls_ref, cnt, blk, alpha_ref, u_piece, v, out, rws, cls, sems, alpha, acc
):
    for c in lists((rws_ref, rws), (cls_ref, cls), (alpha_ref, alpha), sems=sems):
        c.wait()
    forward(1, blk, rws, cls, cnt, v, acc)
    first_sums(1, acc, alpha, u_piece)
    store_pairs(acc, out)


def next_forward_0(
    total_rays,
    rws_ref, cls_ref, cnt, blk, own, other, v_old,
    out, vupd, beta_out,
    rws, cls, sems, acc,
):
    copies = lists((rws_ref, rws), (cls_ref, cls), sems=sems)
    cells = v_old.shape[0]
    beta = jnp.sqrt((own[cells] + other[cells]) / total_rays + EPS)
    beta_out[...] = beta
    inv = 1.0 / beta
    for b in range(cells):
        vupd[b] = (own[b] + other[b]) * inv - beta * v_old[b]
    sq = squares(vupd, cells)
    lanes = lax.broadcasted_iota(jnp.int32, (8, 128), 1)
    sq = jnp.where(lanes == lax.axis_index("col"), sq, 0.0)
    high = sq.astype(BF16).astype(F32)
    out[out.shape[0] - 1] = jnp.concatenate([high, sq - high], axis=0).astype(BF16)
    for c in copies:
        c.wait()
    forward(0, blk, rws, cls, cnt, vupd, acc)
    store_pairs(acc, out)


def next_forward_1(rws_ref, cls_ref, cnt, blk, vupd, out, rws, cls, sems, acc):
    for c in lists((rws_ref, rws), (cls_ref, cls), sems=sems):
        c.wait()
    forward(1, blk, rws, cls, cnt, vupd, acc)
    store_pairs(acc, out)


def new_rays(sum0, sum1, upd, inv=None, ratio=None, old=None):
    for t in range(upd.shape[0] // 2):
        s = sum0[t].astype(F32) + sum1[t].astype(F32)
        for i in range(2):
            x = s[8 * i : 8 * i + 8]
            upd[2 * t + i] = x if old is None else x * inv - ratio * old[2 * t + i]


def begin(cells, message, upd, even, odd):
    message[:cells] = jnp.zeros((cells, 8, 128), F32)
    message[cells] = squares(upd, upd.shape[0])
    spread(upd, even, odd)


def go_on(cells, before, message, upd, even, odd):
    message[:cells] = before[:cells]
    message[cells] = before[cells] + squares(upd, upd.shape[0])
    spread(upd, even, odd)


def first_backward_0(
    cells, rws_ref, cls_ref, cnt, blk, sum0, sum1, upd, message, rws, cls, sems, even, odd
):
    copies = lists((rws_ref, rws), (cls_ref, cls), sems=sems)
    new_rays(sum0, sum1, upd)
    begin(cells, message, upd, even, odd)
    for c in copies:
        c.wait()
    backward(0, blk, rws, cls, cnt, even, odd, message)


def first_backward_1(
    cells, rws_ref, cls_ref, cnt, blk, sum0, sum1, before, upd, message, rws, cls, sems, even, odd
):
    copies = lists((rws_ref, rws), (cls_ref, cls), sems=sems)
    new_rays(sum0, sum1, upd)
    go_on(cells, before, message, upd, even, odd)
    for c in copies:
        c.wait()
    backward(1, blk, rws, cls, cnt, even, odd, message)


def next_backward_0(
    cells, total_cells,
    rws_ref, cls_ref, cnt, blk, sum0, sum1, old, beta,
    message, u_piece, alpha_out,
    rws, cls, sems, even, odd, upd,
):
    copies = lists((rws_ref, rws), (cls_ref, cls), sems=sems)
    last = sum0.shape[0] - 1
    tail = sum0[last].astype(F32) + sum1[last].astype(F32)
    alpha = jnp.sqrt(lane_sum(tail[:8] + tail[8:]) / total_cells + EPS)
    alpha_out[...] = alpha
    new_rays(sum0, sum1, upd, 1.0 / alpha, alpha / beta[...], old)
    begin(cells, message, upd, even, odd)
    base = lax.axis_index("col") * u_piece.shape[0]
    for b in range(u_piece.shape[0]):
        u_piece[b] = even[base + b]
    for c in copies:
        c.wait()
    backward(0, blk, rws, cls, cnt, even, odd, message)


def next_backward_1(
    cells,
    rws_ref, cls_ref, cnt, blk, sum0, sum1, old, beta, alpha, before, u_low,
    message, u_piece,
    rws, cls, sems, even, odd, upd,
):
    copies = lists((rws_ref, rws), (cls_ref, cls), sems=sems)
    new_rays(sum0, sum1, upd, 1.0 / alpha[...], alpha[...] / beta[...], old)
    go_on(cells, before, message, upd, even, odd)
    base = lax.axis_index("col") * u_piece.shape[0]
    for b in range(u_piece.shape[0]):
        u_piece[b] = u_low[b] + odd[base + b]
    for c in copies:
        c.wait()
    backward(1, blk, rws, cls, cnt, even, odd, message)


def last_cells(total_rays, own, other, v_old, alpha, sq, vupd, beta_out):
    cells = v_old.shape[0]
    beta = jnp.sqrt((own[cells] + other[cells]) / total_rays + EPS)
    beta_out[...] = beta
    inv = 1.0 / beta
    scale = beta / alpha[...]
    for b in range(cells):
        vupd[b] = (own[b] + other[b]) * inv - scale * v_old[b]
    sq[...] = squares(vupd, cells)


def finish(
    total_cells,
    phibar_in,
    rhobar_in,
    sq,
    v1,
    v2,
    u_piece,
    x_in,
    w_in,
    beta1,
    alpha1,
    beta2,
    u_out,
    v_out,
    x_out,
    w_out,
    scalars,
):
    alpha2 = jnp.sqrt(sq[...] / total_cells + EPS)
    phibar, rhobar = column(phibar_in), column(rhobar_in)
    steps = []
    for beta, alpha in ((beta1[...], alpha1[...]), (beta2[...], alpha2)):
        rho = jnp.sqrt(rhobar * rhobar + beta * beta)
        cosine, sine = rhobar / rho, beta / rho
        steps.append((cosine * phibar / rho, sine * alpha / rho, 1.0 / alpha))
        rhobar = -cosine * alpha
        phibar = sine * phibar
    half = x_in.shape[1] // 128
    base = lax.axis_index("row") * half
    for b in range(half):
        at = slice(b * 128, (b + 1) * 128)
        x, w = x_in[:, at], w_in[:, at]
        for (along, back, inv), vupd in zip(steps, (v1, v2)):
            v = vupd[base + b] * inv
            x = x + along * w
            w = v - back * w
        v_out[:, at], x_out[:, at], w_out[:, at] = v, x, w
    inv = 1.0 / beta2[...]
    for b in range(u_piece.shape[0]):
        u_out[:, b * 128 : (b + 1) * 128] = u_piece[b] * inv
    rows = lax.broadcasted_iota(jnp.int32, (8, 128), 0)
    lanes = lax.broadcasted_iota(jnp.int32, (8, 128), 1)
    for i, value in enumerate((alpha2, phibar, rhobar)):
        line = jnp.sum(jnp.where(rows == lanes, value, 0.0), axis=0, keepdims=True)
        scalars[i : i + 1, :] = line[:, :8]


def other_core(x):
    return lax.ppermute(x, "row", [(0, 1), (1, 0)])


def column_sum(halves):
    n = lax.axis_size("col")
    steps = [1 << i for i in range((n - 1).bit_length())]
    turned = steps[-1:] + steps[:-1]
    orders = ((steps, turned), (steps, turned))
    xs = list(halves)
    for i in range(len(steps)):
        ys = [
            lax.ppermute(
                x,
                ("row", "col"),
                [(j, j ^ first[i]) for j in range(n)] + [(n + j, n + (j ^ second[i])) for j in range(n)],
            )
            for x, (first, second) in zip(xs, orders)
        ]
        if i == len(steps) - 1:
            return xs[0], ys[0], xs[1], ys[1]
        xs = [(x.astype(F32) + y.astype(F32)).astype(BF16) for x, y in zip(xs, ys)]


def last_sum(x):
    n = lax.axis_size("col")
    m = 1
    while m < n:
        pairs = [(i + n * r, (i ^ m) + n * (1 - r)) for r in (0, 1) for i in range(n)]
        x = x + lax.ppermute(x, ("row", "col"), pairs)
        m *= 2
    return x


def body(
    blocks, block_rows, block_cols, counts, u_rays, v_cells, x_cells, w_cells, alpha, phibar, rhobar
):
    n_row = lax.axis_size("row")
    n_col = lax.axis_size("col")
    pieces = u_rays.shape[1] // 128
    half = v_cells.shape[1] // 128
    rays = pieces * n_col
    cells = half * n_row
    total_rays = float(rays * 128 * n_row)
    total_cells = float(cells * 128 * n_col)
    where = (block_rows, block_cols, counts)
    listed = [
        pltpu.SMEM(block_rows.shape, jnp.int32),
        pltpu.SMEM(block_cols.shape, jnp.int32),
        pltpu.SemaphoreType.DMA((3,)),
    ]
    ray_acc = pltpu.VMEM((rays, 8, 128), F32)
    half_upd = shape(rays // 2, 8, 128)
    half_rays = shape(rays // 4, 16, 128, dtype=BF16)
    with_tail = shape(rays // 4 + 1, 16, 128, dtype=BF16)
    group, tile = shape(cells, 8, 128), shape(8, 128)
    sent = shape(cells + 1, 8, 128)
    piece = shape(pieces, 8, 128)
    flops = 2 * blocks.shape[2] * 64 * 128 * 8
    cost = pl.CostEstimate(flops=flops, bytes_accessed=2**21, transcendentals=0)

    def product(kernel, out_shape, args, *scratch):
        return call(kernel, out_shape, [VMEM] * len(args), listed + list(scratch), cost)(*args)

    own = call(
        load,
        shape(*v_cells.shape),
        [HBM],
        [pltpu.SemaphoreType.DMA],
        pl.CostEstimate(flops=5 * 10**9, bytes_accessed=1, transcendentals=0),
    )(v_cells)
    v_other = other_core(own)
    blk = blocks.reshape(blocks.shape[2:])
    operator = (*where, blk)
    first = (*operator, alpha, u_rays)
    alpha_copy = pltpu.SMEM(alpha.shape, F32)
    part0, v0 = product(
        first_forward_0, (half_rays, group), (*first, own, v_other), alpha_copy, ray_acc
    )
    part1 = product(first_forward_1, half_rays, (*first, v0), alpha_copy, ray_acc)
    sums = column_sum((part0, part1))
    upd0, message = product(
        functools.partial(first_backward_0, cells),
        (half_upd, sent),
        (*operator, *sums[:2]),
        ray_acc,
        ray_acc,
    )
    upd1, message = product(
        functools.partial(first_backward_1, cells),
        (half_upd, sent),
        (*operator, *sums[2:], message),
        ray_acc,
        ray_acc,
    )
    part0, v1, beta1 = product(
        functools.partial(next_forward_0, total_rays),
        (with_tail, group, tile),
        (*operator, message, other_core(message), v0),
        ray_acc,
    )
    part1 = product(next_forward_1, half_rays, (*operator, v1), ray_acc)
    sums = column_sum((part0, part1))
    upd_copy = pltpu.VMEM((rays // 2, 8, 128), F32)
    message, u_low, alpha1 = product(
        functools.partial(next_backward_0, cells, total_cells),
        (sent, piece, tile),
        (*operator, *sums[:2], upd0, beta1),
        ray_acc,
        ray_acc,
        upd_copy,
    )
    message, u_piece = product(
        functools.partial(next_backward_1, cells),
        (sent, piece),
        (*operator, *sums[2:], upd1, beta1, alpha1, message, u_low),
        ray_acc,
        ray_acc,
        upd_copy,
    )
    sq, v2, beta2 = call(
        functools.partial(last_cells, total_rays),
        (shape(8, 128), shape(cells, 8, 128), shape(8, 128)),
        [VMEM] * 4,
    )(message, other_core(message), v1, alpha1)
    sq = last_sum(sq)
    flat = shape(*v_cells.shape)
    return call(
        functools.partial(finish, total_cells),
        (shape(*u_rays.shape), flat, flat, flat, shape(3, 8)),
        [SMEM] * 2 + [VMEM] * 9,
    )(phibar, rhobar, sq, v1, v2, u_piece, x_cells, w_cells, beta1, alpha1, beta2)


def solution(mesh):
    placed = (
        P(("region", "row"), "col", None, None, None),
        P(("region", "row"), "col", None),
        P(("region", "row"), "col", None),
        P(("region", "row"), "col"),
        P(None, ("region", "row", "col")),
        P(None, ("region", "col", "row")),
        P(None, ("region", "col", "row")),
        P(None, ("region", "col", "row")),
        P("region"),
        P("region"),
        P("region"),
    )
    return jax.shard_map(
        body,
        mesh=mesh,
        in_specs=placed,
        out_specs=(
            P(None, ("region", "row", "col")),
            P(None, ("region", "col", "row")),
            P(None, ("region", "col", "row")),
            P(None, ("region", "col", "row")),
            P(None, "region"),
        ),
        check_vma=False,
    )
```

```python
import functools

import jax
import jax.numpy as jnp
from jax import lax
from jax.experimental import pallas as pl
from jax.experimental.pallas import tpu as pltpu
from jax.sharding import PartitionSpec as P

ITERS = 2
EPS = 1e-6
F32 = jnp.float32
BF16 = jnp.bfloat16
SMEM = pl.BlockSpec(memory_space=pltpu.SMEM)
HBM = pl.BlockSpec(memory_space=pltpu.HBM)
VMEM = pl.BlockSpec(memory_space=pltpu.VMEM)


def call(kernel, out_shape, in_specs, scratch=(), cost=None):
    return pl.pallas_call(
        kernel,
        out_shape=out_shape,
        in_specs=in_specs,
        out_specs=jax.tree.map(lambda _: VMEM, out_shape),
        scratch_shapes=list(scratch),
        cost_estimate=cost,
        compiler_params=pltpu.CompilerParams(vmem_limit_bytes=48 * 1024 * 1024),
    )


def shape(*dims, dtype=F32):
    return jax.ShapeDtypeStruct(dims, dtype)


def lists(*pairs, sems):
    copies = [pltpu.make_async_copy(*pair, sems.at[i]) for i, pair in enumerate(pairs)]
    for copy in copies:
        copy.start()
    return copies


def used(count, k, prod):
    return jnp.where(count > k, prod, 0.0)


def forward(blk, rws, cls, cnt, v_ref, acc_ref):
    count = jnp.broadcast_to(cnt[...], (8, 128))
    acc_ref[...] = jnp.zeros_like(acc_ref)
    for k in range(0, blk.shape[0], 2):
        pair = jnp.concatenate([v_ref[cls[0, 0, k]], v_ref[cls[0, 0, k + 1]]], axis=0)
        a = blk[k : k + 2].reshape(256, 128)
        prod = lax.dot_general(
            pair.astype(BF16), a, (((1,), (1,)), ((), ())), preferred_element_type=F32
        )
        acc_ref[rws[0, 0, k]] += used(count, k, prod[:8, :128])
        acc_ref[rws[0, 0, k + 1]] += used(count, k + 1, prod[8:, 128:])


def backward(blk, rws, cls, cnt, u_ref, accs, out):
    count = jnp.broadcast_to(cnt[...], (8, 128))
    for acc in accs:
        acc[...] = jnp.zeros_like(acc)
    zero = jnp.zeros((8, 128), F32)
    for k in range(0, blk.shape[0], 2):
        u0 = jnp.concatenate([u_ref[rws[0, 0, k]], zero], axis=0).astype(BF16)
        u1 = jnp.concatenate([zero, u_ref[rws[0, 0, k + 1]]], axis=0).astype(BF16)
        a = blk[k : k + 2].reshape(256, 128)
        prod = jnp.dot(jnp.concatenate([u0, u1], axis=1), a, preferred_element_type=F32)
        accs[k % len(accs)][cls[0, 0, k]] += used(count, k, prod[:8])
        accs[(k + 1) % len(accs)][cls[0, 0, k + 1]] += used(count, k + 1, prod[8:])
    for c in range(accs[0].shape[0]):
        out[c] = functools.reduce(jnp.add, [acc[c] for acc in accs])


def column(ref):
    rows = lax.broadcasted_iota(jnp.int32, (8, 128), 0)
    out = jnp.zeros((8, 128), F32)
    for s in range(8):
        out = jnp.where(rows == s, ref[s], out)
    return out


def lane_sum(x):
    return jnp.broadcast_to(jnp.sum(x, axis=1, keepdims=True), (8, 128))


def squares(ref, blocks):
    totals = [jnp.zeros((8, 128), F32)] * 4
    for b in range(blocks):
        totals[b % 4] = totals[b % 4] + ref[b] * ref[b]
    return lane_sum((totals[0] + totals[1]) + (totals[2] + totals[3]))


def store_pairs(acc_ref, outs):
    half = acc_ref.shape[0] // 4
    for b in range(2 * half):
        pair = jnp.concatenate([acc_ref[2 * b], acc_ref[2 * b + 1]], axis=0)
        outs[b // half][b % half] = pair.astype(BF16)


def place_halves(own, other, out_ref):
    half = own.shape[1] // 128
    row = lax.axis_index("row")
    for b in range(half):
        out_ref[row * half + b] = own[:, b * 128 : (b + 1) * 128]
        out_ref[(1 - row) * half + b] = other[:, b * 128 : (b + 1) * 128]


def load(own_hbm, own, sem):
    copy = pltpu.make_async_copy(own_hbm, own, sem)
    copy.start()
    copy.wait()


def first_forward(
    rws_ref, cls_ref, cnt, blk, alpha_ref, own, other, u_piece,
    out0, out1, v_out,
    rws, cls, sems, alpha, acc,
):
    copies = lists((rws_ref, rws), (cls_ref, cls), (alpha_ref, alpha), sems=sems)
    place_halves(own, other, v_out)
    for c in copies:
        c.wait()
    forward(blk, rws, cls, cnt, v_out, acc)
    pieces = u_piece.shape[1] // 128
    base = lax.axis_index("col") * pieces
    a = column(alpha)
    for b in range(pieces):
        acc[base + b] -= a * u_piece[:, b * 128 : (b + 1) * 128]
    store_pairs(acc, (out0, out1))


def pair_sums(pairs, a0, a1, b0, b1):
    half = pairs // 2
    for b in range(pairs):
        one, two = (a0, a1) if b < half else (b0, b1)
        yield one[b % half].astype(F32) + two[b % half].astype(F32)


def first_backward(rws_ref, cls_ref, cnt, blk, sums0, sums1, sums2, sums3, upd, message, rws, cls, sems, *accs):
    copies = lists((rws_ref, rws), (cls_ref, cls), sems=sems)
    blocks = upd.shape[0]
    for b, s in enumerate(pair_sums(blocks // 2, sums0, sums1, sums2, sums3)):
        upd[2 * b] = s[:8]
        upd[2 * b + 1] = s[8:]
    cells = message.shape[0] - 1
    message[cells] = squares(upd, blocks)
    for c in copies:
        c.wait()
    backward(blk, rws, cls, cnt, upd, accs, message)


def next_forward(
    total_rays,
    rws_ref, cls_ref, cnt, blk, own, other, v_old,
    out0, out1, vupd, beta_out,
    rws, cls, sems, acc,
):
    copies = lists((rws_ref, rws), (cls_ref, cls), sems=sems)
    cells = v_old.shape[0]
    beta = jnp.sqrt((own[cells] + other[cells]) / total_rays + EPS)
    beta_out[...] = beta
    inv = 1.0 / beta
    for b in range(cells):
        vupd[b] = (own[b] + other[b]) * inv - beta * v_old[b]
    rays = acc.shape[0]
    sq = squares(vupd, cells)
    lanes = lax.broadcasted_iota(jnp.int32, (8, 128), 1)
    sq = jnp.where(lanes == lax.axis_index("col"), sq, 0.0)
    high = sq.astype(BF16).astype(F32)
    out0[rays // 4] = jnp.concatenate([high, sq - high], axis=0).astype(BF16)
    for c in copies:
        c.wait()
    forward(blk, rws, cls, cnt, vupd, acc)
    store_pairs(acc, (out0, out1))


def next_backward(
    total_cells, pieces,
    rws_ref, cls_ref, cnt, blk, sums0, sums1, sums2, sums3, old, beta,
    message, u_piece, alpha_out,
    rws, cls, sems, upd, *accs,
):
    copies = lists((rws_ref, rws), (cls_ref, cls), sems=sems)
    blocks = upd.shape[0]
    tail = sums0[blocks // 4].astype(F32) + sums1[blocks // 4].astype(F32)
    alpha = jnp.sqrt(lane_sum(tail[:8] + tail[8:]) / total_cells + EPS)
    alpha_out[...] = alpha
    inv = 1.0 / alpha
    ratio = alpha / beta[...]
    for b, s in enumerate(pair_sums(blocks // 2, sums0, sums1, sums2, sums3)):
        upd[2 * b] = s[:8] * inv - ratio * old[2 * b]
        upd[2 * b + 1] = s[8:] * inv - ratio * old[2 * b + 1]
    cells = message.shape[0] - 1
    message[cells] = squares(upd, blocks)
    base = lax.axis_index("col") * pieces
    for b in range(pieces):
        u_piece[b] = upd[base + b]
    for c in copies:
        c.wait()
    backward(blk, rws, cls, cnt, upd, accs, message)


def last_cells(total_rays, own, other, v_old, alpha, sq, vupd, beta_out):
    cells = v_old.shape[0]
    beta = jnp.sqrt((own[cells] + other[cells]) / total_rays + EPS)
    beta_out[...] = beta
    inv = 1.0 / beta
    scale = beta / alpha[...]
    for b in range(cells):
        vupd[b] = (own[b] + other[b]) * inv - scale * v_old[b]
    sq[...] = squares(vupd, cells)


def settle(
    phibar_in, rhobar_in, v1, u_piece, x_in, w_in, beta1, alpha1, beta2,
    u_out, x_out, w_mid, factors,
):
    phibar, rhobar, beta, alpha = column(phibar_in), column(rhobar_in), beta1[...], alpha1[...]
    rho = jnp.sqrt(rhobar * rhobar + beta * beta)
    cosine, sine = rhobar / rho, beta / rho
    along, back, inv = cosine * phibar / rho, sine * alpha / rho, 1.0 / alpha
    rhobar, phibar = -cosine * alpha, sine * phibar
    beta = beta2[...]
    rho = jnp.sqrt(rhobar * rhobar + beta * beta)
    cosine, sine = rhobar / rho, beta / rho
    along2 = cosine * phibar / rho
    factors[0], factors[1], factors[2] = sine / rho, -cosine, sine * phibar
    half = x_in.shape[1] // 128
    base = lax.axis_index("row") * half
    for b in range(half):
        at = slice(b * 128, (b + 1) * 128)
        w_old = w_in[:, at]
        w = v1[base + b] * inv - back * w_old
        x_out[:, at] = x_in[:, at] + along * w_old + along2 * w
        w_mid[:, at] = w
    inv = 1.0 / beta
    for b in range(u_piece.shape[0]):
        u_out[:, b * 128 : (b + 1) * 128] = u_piece[b] * inv


def finish(total_cells, sq, v2, w_mid, factors, v_out, w_out, scalars):
    alpha = jnp.sqrt(sq[...] / total_cells + EPS)
    inv, back = 1.0 / alpha, factors[0] * alpha
    half = v_out.shape[1] // 128
    base = lax.axis_index("row") * half
    for b in range(half):
        at = slice(b * 128, (b + 1) * 128)
        v = v2[base + b] * inv
        v_out[:, at], w_out[:, at] = v, v - back * w_mid[:, at]
    rows = lax.broadcasted_iota(jnp.int32, (8, 128), 0)
    lanes = lax.broadcasted_iota(jnp.int32, (8, 128), 1)
    for i, value in enumerate((alpha, factors[2], factors[1] * alpha)):
        line = jnp.sum(jnp.where(rows == lanes, value, 0.0), axis=0, keepdims=True)
        scalars[i : i + 1, :] = line[:, :8]


def other_core(x):
    return lax.ppermute(x, "row", [(0, 1), (1, 0)])


def column_sum(halves):
    n = lax.axis_size("col")
    steps = [1 << i for i in range((n - 1).bit_length())]
    turned = steps[-1:] + steps[:-1]
    orders = ((steps, turned), (steps, turned))
    xs = list(halves)
    for i in range(len(steps)):
        ys = [
            lax.ppermute(
                x,
                ("row", "col"),
                [(j, j ^ first[i]) for j in range(n)] + [(n + j, n + (j ^ second[i])) for j in range(n)],
            )
            for x, (first, second) in zip(xs, orders)
        ]
        if i == len(steps) - 1:
            return xs[0], ys[0], xs[1], ys[1]
        xs = [(x.astype(F32) + y.astype(F32)).astype(BF16) for x, y in zip(xs, ys)]


def last_sum(x):
    n = lax.axis_size("col")
    m = 1
    while m < n:
        pairs = [(i + n * r, (i ^ m) + n * (1 - r)) for r in (0, 1) for i in range(n)]
        x = x + lax.ppermute(x, ("row", "col"), pairs)
        m *= 2
    return x


def body(
    blocks, block_rows, block_cols, counts, u_rays, v_cells, x_cells, w_cells, alpha, phibar, rhobar
):
    n_row = lax.axis_size("row")
    n_col = lax.axis_size("col")
    pieces = u_rays.shape[1] // 128
    half = v_cells.shape[1] // 128
    rays = pieces * n_col
    cells = half * n_row
    total_rays = float(rays * 128 * n_row)
    total_cells = float(cells * 128 * n_col)
    where = (block_rows, block_cols, counts)
    listed = [
        pltpu.SMEM(block_rows.shape, jnp.int32),
        pltpu.SMEM(block_cols.shape, jnp.int32),
        pltpu.SemaphoreType.DMA((3,)),
    ]
    ray_acc = pltpu.VMEM((rays, 8, 128), F32)
    cell_accs = [pltpu.VMEM((cells, 8, 128), F32)] * 4
    own = call(
        load,
        shape(*v_cells.shape),
        [HBM],
        [pltpu.SemaphoreType.DMA],
        pl.CostEstimate(flops=5 * 10**9, bytes_accessed=1, transcendentals=0),
    )(v_cells)
    v_other = other_core(own)
    blk = blocks.reshape(blocks.shape[2:])
    operator = (*where, blk)
    half_rays = shape(rays // 4, 16, 128, dtype=BF16)
    *part, v0 = call(
        first_forward,
        (half_rays, half_rays, shape(cells, 8, 128)),
        [VMEM] * 8,
        listed + [pltpu.SMEM(alpha.shape, F32), ray_acc],
    )(*operator, alpha, own, v_other, u_rays)
    sums = column_sum(part)
    upd1, message = call(
        first_backward,
        (shape(rays, 8, 128), shape(cells + 1, 8, 128)),
        [VMEM] * 8,
        listed + cell_accs,
    )(*operator, *sums)
    *part, v1, beta1 = call(
        functools.partial(next_forward, total_rays),
        (shape(rays // 4 + 1, 16, 128, dtype=BF16), half_rays, shape(cells, 8, 128), shape(8, 128)),
        [VMEM] * 7,
        listed + [ray_acc],
    )(*operator, message, other_core(message), v0)
    sums = column_sum(part)
    message, u_piece, alpha1 = call(
        functools.partial(next_backward, total_cells, pieces),
        (shape(cells + 1, 8, 128), shape(pieces, 8, 128), shape(8, 128)),
        [VMEM] * 10,
        listed + [pltpu.VMEM((rays, 8, 128), F32)] + cell_accs,
    )(*operator, *sums, upd1, beta1)
    sq, v2, beta2 = call(
        functools.partial(last_cells, total_rays),
        (shape(8, 128), shape(cells, 8, 128), shape(8, 128)),
        [VMEM] * 4,
    )(message, other_core(message), v1, alpha1)
    sq = last_sum(sq)
    flat = shape(*v_cells.shape)
    u, x, w_mid, factors = call(
        settle,
        (shape(*u_rays.shape), flat, flat, shape(3, 8, 128)),
        [SMEM] * 2 + [VMEM] * 7,
        (),
        pl.CostEstimate(flops=10**6, bytes_accessed=3 * 10**6, transcendentals=0),
    )(phibar, rhobar, v1, u_piece, x_cells, w_cells, beta1, alpha1, beta2)
    v, w, scalars = call(
        functools.partial(finish, total_cells), (flat, flat, shape(3, 8)), [VMEM] * 4
    )(sq, v2, w_mid, factors)
    return u, v, x, w, scalars


def solution(mesh):
    placed = (
        P(("region", "row"), "col", None, None, None),
        P(("region", "row"), "col", None),
        P(("region", "row"), "col", None),
        P(("region", "row"), "col"),
        P(None, ("region", "row", "col")),
        P(None, ("region", "col", "row")),
        P(None, ("region", "col", "row")),
        P(None, ("region", "col", "row")),
        P("region"),
        P("region"),
        P("region"),
    )
    return jax.shard_map(
        body,
        mesh=mesh,
        in_specs=placed,
        out_specs=(
            P(None, ("region", "row", "col")),
            P(None, ("region", "col", "row")),
            P(None, ("region", "col", "row")),
            P(None, ("region", "col", "row")),
            P(None, "region"),
        ),
        check_vma=False,
    )
```

```python
import functools

import jax
import jax.numpy as jnp
from jax import lax
from jax.experimental import pallas as pl
from jax.experimental.pallas import tpu as pltpu
from jax.sharding import PartitionSpec as P

ITERS = 2
EPS = 1e-6
CUT = 16
F32 = jnp.float32
BF16 = jnp.bfloat16
SMEM = pl.BlockSpec(memory_space=pltpu.SMEM)
HBM = pl.BlockSpec(memory_space=pltpu.HBM)
VMEM = pl.BlockSpec(memory_space=pltpu.VMEM)


def call(kernel, out_shape, in_specs, scratch=(), cost=None):
    return pl.pallas_call(
        kernel,
        out_shape=out_shape,
        in_specs=in_specs,
        out_specs=jax.tree.map(lambda _: VMEM, out_shape),
        scratch_shapes=list(scratch),
        cost_estimate=cost,
        compiler_params=pltpu.CompilerParams(vmem_limit_bytes=48 * 1024 * 1024),
    )


def shape(*dims, dtype=F32):
    return jax.ShapeDtypeStruct(dims, dtype)


def lists(*pairs, sems):
    copies = [pltpu.make_async_copy(*pair, sems.at[i]) for i, pair in enumerate(pairs)]
    for copy in copies:
        copy.start()
    return copies


def used(count, k, prod):
    return jnp.where(count > k, prod, 0.0)


def forward(blk, rws, cls, cnt, v_ref, acc_ref, turned=False):
    count = jnp.broadcast_to(cnt[...], (8, 128))
    acc_ref[...] = jnp.zeros_like(acc_ref)
    for k in range(0, blk.shape[0], 2):
        pair = jnp.concatenate([v_ref[cls[0, 0, k]], v_ref[cls[0, 0, k + 1]]], axis=0)
        if turned:
            a = jnp.concatenate([blk[k], blk[k + 1]], axis=1)
            prod = jnp.dot(pair.astype(BF16), a, preferred_element_type=F32)
        else:
            a = blk[k : k + 2].reshape(256, 128)
            prod = lax.dot_general(
                pair.astype(BF16), a, (((1,), (1,)), ((), ())), preferred_element_type=F32
            )
        acc_ref[rws[0, 0, k]] += used(count, k, prod[:8, :128])
        acc_ref[rws[0, 0, k + 1]] += used(count, k + 1, prod[8:, 128:])


def backward(blk, rws, cls, cnt, u_ref, accs, out):
    count = jnp.broadcast_to(cnt[...], (8, 128))
    for acc in accs:
        acc[...] = jnp.zeros_like(acc)
    zero = jnp.zeros((8, 128), F32)
    for k in range(0, blk.shape[0], 2):
        u0 = jnp.concatenate([u_ref[rws[0, 0, k]], zero], axis=0).astype(BF16)
        u1 = jnp.concatenate([zero, u_ref[rws[0, 0, k + 1]]], axis=0).astype(BF16)
        a = blk[k : k + 2].reshape(256, 128)
        prod = jnp.dot(jnp.concatenate([u0, u1], axis=1), a, preferred_element_type=F32)
        accs[k % len(accs)][cls[0, 0, k]] += used(count, k, prod[:8])
        accs[(k + 1) % len(accs)][cls[0, 0, k + 1]] += used(count, k + 1, prod[8:])
    for c in range(accs[0].shape[0]):
        out[c] = functools.reduce(jnp.add, [acc[c] for acc in accs])


def column(ref):
    rows = lax.broadcasted_iota(jnp.int32, (8, 128), 0)
    out = jnp.zeros((8, 128), F32)
    for s in range(8):
        out = jnp.where(rows == s, ref[s], out)
    return out


def lane_sum(x):
    return jnp.broadcast_to(jnp.sum(x, axis=1, keepdims=True), (8, 128))


def squares(ref, blocks):
    totals = [jnp.zeros((8, 128), F32)] * 4
    for b in range(blocks):
        totals[b % 4] = totals[b % 4] + ref[b] * ref[b]
    return lane_sum((totals[0] + totals[1]) + (totals[2] + totals[3]))


def first_part(pairs):
    return pairs * CUT // 32


def store_pairs(acc_ref, outs):
    cut = first_part(acc_ref.shape[0] // 2)
    for b in range(acc_ref.shape[0] // 2):
        pair = jnp.concatenate([acc_ref[2 * b], acc_ref[2 * b + 1]], axis=0)
        outs[int(b >= cut)][b - cut * int(b >= cut)] = pair.astype(BF16)


def place_halves(own, other, out_ref):
    half = own.shape[1] // 128
    row = lax.axis_index("row")
    for b in range(half):
        out_ref[row * half + b] = own[:, b * 128 : (b + 1) * 128]
        out_ref[(1 - row) * half + b] = other[:, b * 128 : (b + 1) * 128]


def load(own_hbm, own, sem):
    copy = pltpu.make_async_copy(own_hbm, own, sem)
    copy.start()
    copy.wait()


def turn(blk, out):
    for k in range(blk.shape[0]):
        out[k] = blk[k].T


def first_forward(
    rws_ref, cls_ref, cnt, blk, alpha_ref, own, other, u_piece,
    out0, out1, v_out,
    rws, cls, sems, alpha, acc,
):
    copies = lists((rws_ref, rws), (cls_ref, cls), (alpha_ref, alpha), sems=sems)
    place_halves(own, other, v_out)
    for c in copies:
        c.wait()
    forward(blk, rws, cls, cnt, v_out, acc)
    pieces = u_piece.shape[1] // 128
    base = lax.axis_index("col") * pieces
    a = column(alpha)
    for b in range(pieces):
        acc[base + b] -= a * u_piece[:, b * 128 : (b + 1) * 128]
    store_pairs(acc, (out0, out1))


def pair_sums(pairs, a0, a1, b0, b1):
    cut = first_part(pairs)
    for b in range(pairs):
        one, two, at = (a0, a1, b) if b < cut else (b0, b1, b - cut)
        yield one[at].astype(F32) + two[at].astype(F32)


def first_backward(rws_ref, cls_ref, cnt, blk, sums0, sums1, sums2, sums3, upd, message, rws, cls, sems, *accs):
    copies = lists((rws_ref, rws), (cls_ref, cls), sems=sems)
    blocks = upd.shape[0]
    for b, s in enumerate(pair_sums(blocks // 2, sums0, sums1, sums2, sums3)):
        upd[2 * b] = s[:8]
        upd[2 * b + 1] = s[8:]
    cells = message.shape[0] - 1
    message[cells] = squares(upd, blocks)
    for c in copies:
        c.wait()
    backward(blk, rws, cls, cnt, upd, accs, message)


def next_forward(
    total_rays,
    rws_ref, cls_ref, cnt, blk, own, other, v_old,
    out0, out1, vupd, beta_out,
    rws, cls, sems, acc,
):
    copies = lists((rws_ref, rws), (cls_ref, cls), sems=sems)
    cells = v_old.shape[0]
    beta = jnp.sqrt((own[cells] + other[cells]) / total_rays + EPS)
    beta_out[...] = beta
    inv = 1.0 / beta
    for b in range(cells):
        vupd[b] = (own[b] + other[b]) * inv - beta * v_old[b]
    rays = acc.shape[0]
    sq = squares(vupd, cells)
    lanes = lax.broadcasted_iota(jnp.int32, (8, 128), 1)
    sq = jnp.where(lanes == lax.axis_index("col"), sq, 0.0)
    high = sq.astype(BF16).astype(F32)
    out0[out0.shape[0] - 1] = jnp.concatenate([high, sq - high], axis=0).astype(BF16)
    for c in copies:
        c.wait()
    forward(blk, rws, cls, cnt, vupd, acc, turned=True)
    store_pairs(acc, (out0, out1))


def next_backward(
    total_cells, pieces,
    rws_ref, cls_ref, cnt, blk, sums0, sums1, sums2, sums3, old, beta,
    message, u_piece, alpha_out,
    rws, cls, sems, upd, *accs,
):
    copies = lists((rws_ref, rws), (cls_ref, cls), sems=sems)
    blocks = upd.shape[0]
    tail = sums0[sums0.shape[0] - 1].astype(F32) + sums1[sums1.shape[0] - 1].astype(F32)
    alpha = jnp.sqrt(lane_sum(tail[:8] + tail[8:]) / total_cells + EPS)
    alpha_out[...] = alpha
    inv = 1.0 / alpha
    ratio = alpha / beta[...]
    for b, s in enumerate(pair_sums(blocks // 2, sums0, sums1, sums2, sums3)):
        upd[2 * b] = s[:8] * inv - ratio * old[2 * b]
        upd[2 * b + 1] = s[8:] * inv - ratio * old[2 * b + 1]
    cells = message.shape[0] - 1
    message[cells] = squares(upd, blocks)
    base = lax.axis_index("col") * pieces
    for b in range(pieces):
        u_piece[b] = upd[base + b]
    for c in copies:
        c.wait()
    backward(blk, rws, cls, cnt, upd, accs, message)


def last_cells(total_rays, own, other, v_old, alpha, sq, vupd, beta_out):
    cells = v_old.shape[0]
    beta = jnp.sqrt((own[cells] + other[cells]) / total_rays + EPS)
    beta_out[...] = beta
    inv = 1.0 / beta
    scale = beta / alpha[...]
    for b in range(cells):
        vupd[b] = (own[b] + other[b]) * inv - scale * v_old[b]
    sq[...] = squares(vupd, cells)


def settle(
    phibar_in, rhobar_in, v1, u_piece, x_in, w_in, beta1, alpha1, beta2,
    u_out, x_out, w_mid, factors,
):
    phibar, rhobar, beta, alpha = column(phibar_in), column(rhobar_in), beta1[...], alpha1[...]
    rho = jnp.sqrt(rhobar * rhobar + beta * beta)
    cosine, sine = rhobar / rho, beta / rho
    along, back, inv = cosine * phibar / rho, sine * alpha / rho, 1.0 / alpha
    rhobar, phibar = -cosine * alpha, sine * phibar
    beta = beta2[...]
    rho = jnp.sqrt(rhobar * rhobar + beta * beta)
    cosine, sine = rhobar / rho, beta / rho
    along2 = cosine * phibar / rho
    factors[0], factors[1], factors[2] = sine / rho, -cosine, sine * phibar
    half = x_in.shape[1] // 128
    base = lax.axis_index("row") * half
    for b in range(half):
        at = slice(b * 128, (b + 1) * 128)
        w_old = w_in[:, at]
        w = v1[base + b] * inv - back * w_old
        x_out[:, at] = x_in[:, at] + along * w_old + along2 * w
        w_mid[:, at] = w
    inv = 1.0 / beta
    for b in range(u_piece.shape[0]):
        u_out[:, b * 128 : (b + 1) * 128] = u_piece[b] * inv


def finish(total_cells, sq, v2, w_mid, factors, v_out, w_out, scalars):
    alpha = jnp.sqrt(sq[...] / total_cells + EPS)
    inv, back = 1.0 / alpha, factors[0] * alpha
    half = v_out.shape[1] // 128
    base = lax.axis_index("row") * half
    for b in range(half):
        at = slice(b * 128, (b + 1) * 128)
        v = v2[base + b] * inv
        v_out[:, at], w_out[:, at] = v, v - back * w_mid[:, at]
    rows = lax.broadcasted_iota(jnp.int32, (8, 128), 0)
    lanes = lax.broadcasted_iota(jnp.int32, (8, 128), 1)
    for i, value in enumerate((alpha, factors[2], factors[1] * alpha)):
        line = jnp.sum(jnp.where(rows == lanes, value, 0.0), axis=0, keepdims=True)
        scalars[i : i + 1, :] = line[:, :8]


def other_core(x):
    return lax.ppermute(x, "row", [(0, 1), (1, 0)])


def column_sum(halves, held=None):
    n = lax.axis_size("col")
    steps = [1 << i for i in range((n - 1).bit_length())]
    turned = steps[-1:] + steps[:-1]
    orders = ((steps, turned), (steps, turned))
    xs = list(halves)
    for i in range(len(steps)):
        if held is not None and i == len(steps) - 1:
            xs[1], held = lax.optimization_barrier((xs[1], held))
        ys = [
            lax.ppermute(
                x,
                ("row", "col"),
                [(j, j ^ first[i]) for j in range(n)] + [(n + j, n + (j ^ second[i])) for j in range(n)],
            )
            for x, (first, second) in zip(xs, orders)
        ]
        if i == len(steps) - 1:
            return (xs[0], ys[0], xs[1], ys[1]), held
        xs = [(x.astype(F32) + y.astype(F32)).astype(BF16) for x, y in zip(xs, ys)]


def last_sum(x):
    n = lax.axis_size("col")
    m = 1
    while m < n:
        pairs = [(i + n * r, (i ^ m) + n * (1 - r)) for r in (0, 1) for i in range(n)]
        x = x + lax.ppermute(x, ("row", "col"), pairs)
        m *= 2
    return x


def body(
    blocks, block_rows, block_cols, counts, u_rays, v_cells, x_cells, w_cells, alpha, phibar, rhobar
):
    n_row = lax.axis_size("row")
    n_col = lax.axis_size("col")
    pieces = u_rays.shape[1] // 128
    half = v_cells.shape[1] // 128
    rays = pieces * n_col
    cells = half * n_row
    total_rays = float(rays * 128 * n_row)
    total_cells = float(cells * 128 * n_col)
    where = (block_rows, block_cols, counts)
    listed = [
        pltpu.SMEM(block_rows.shape, jnp.int32),
        pltpu.SMEM(block_cols.shape, jnp.int32),
        pltpu.SemaphoreType.DMA((3,)),
    ]
    ray_acc = pltpu.VMEM((rays, 8, 128), F32)
    cell_accs = [pltpu.VMEM((cells, 8, 128), F32)] * 4
    own = call(
        load,
        shape(*v_cells.shape),
        [HBM],
        [pltpu.SemaphoreType.DMA],
        pl.CostEstimate(flops=5 * 10**9, bytes_accessed=1, transcendentals=0),
    )(v_cells)
    v_other = other_core(own)
    blk = blocks.reshape(blocks.shape[2:])
    operator = (*where, blk)
    cut = first_part(rays // 2)
    rest = shape(rays // 2 - cut, 16, 128, dtype=BF16)
    *part, v0 = call(
        first_forward,
        (shape(cut, 16, 128, dtype=BF16), rest, shape(cells, 8, 128)),
        [VMEM] * 8,
        listed + [pltpu.SMEM(alpha.shape, F32), ray_acc],
    )(*operator, alpha, own, v_other, u_rays)
    sums, held = column_sum(part, blk)
    turned = call(
        turn,
        shape(*blk.shape, dtype=BF16),
        [VMEM],
        (),
        pl.CostEstimate(flops=10**6, bytes_accessed=4 * 10**6, transcendentals=0),
    )(held)
    blk, turned = lax.optimization_barrier((blk, turned))
    operator = (*where, blk)
    upd1, message = call(
        first_backward,
        (shape(rays, 8, 128), shape(cells + 1, 8, 128)),
        [VMEM] * 8,
        listed + cell_accs,
    )(*operator, *sums)
    *part, v1, beta1 = call(
        functools.partial(next_forward, total_rays),
        (shape(cut + 1, 16, 128, dtype=BF16), rest, shape(cells, 8, 128), shape(8, 128)),
        [VMEM] * 7,
        listed + [ray_acc],
    )(*where, turned, message, other_core(message), v0)
    sums, _ = column_sum(part)
    message, u_piece, alpha1 = call(
        functools.partial(next_backward, total_cells, pieces),
        (shape(cells + 1, 8, 128), shape(pieces, 8, 128), shape(8, 128)),
        [VMEM] * 10,
        listed + [pltpu.VMEM((rays, 8, 128), F32)] + cell_accs,
    )(*operator, *sums, upd1, beta1)
    sq, v2, beta2 = call(
        functools.partial(last_cells, total_rays),
        (shape(8, 128), shape(cells, 8, 128), shape(8, 128)),
        [VMEM] * 4,
    )(message, other_core(message), v1, alpha1)
    sq = last_sum(sq)
    flat = shape(*v_cells.shape)
    u, x, w_mid, factors = call(
        settle,
        (shape(*u_rays.shape), flat, flat, shape(3, 8, 128)),
        [SMEM] * 2 + [VMEM] * 7,
        (),
        pl.CostEstimate(flops=10**6, bytes_accessed=3 * 10**6, transcendentals=0),
    )(phibar, rhobar, v1, u_piece, x_cells, w_cells, beta1, alpha1, beta2)
    v, w, scalars = call(
        functools.partial(finish, total_cells), (flat, flat, shape(3, 8)), [VMEM] * 4
    )(sq, v2, w_mid, factors)
    return u, v, x, w, scalars


def solution(mesh):
    placed = (
        P(("region", "row"), "col", None, None, None),
        P(("region", "row"), "col", None),
        P(("region", "row"), "col", None),
        P(("region", "row"), "col"),
        P(None, ("region", "row", "col")),
        P(None, ("region", "col", "row")),
        P(None, ("region", "col", "row")),
        P(None, ("region", "col", "row")),
        P("region"),
        P("region"),
        P("region"),
    )
    return jax.shard_map(
        body,
        mesh=mesh,
        in_specs=placed,
        out_specs=(
            P(None, ("region", "row", "col")),
            P(None, ("region", "col", "row")),
            P(None, ("region", "col", "row")),
            P(None, ("region", "col", "row")),
            P(None, "region"),
        ),
        check_vma=False,
    )
```

```python
import functools

import jax
import jax.numpy as jnp
from jax import lax
from jax.experimental import pallas as pl
from jax.experimental.pallas import tpu as pltpu
from jax.sharding import PartitionSpec as P

ITERS = 2
EPS = 1e-6
F32 = jnp.float32
BF16 = jnp.bfloat16
SMEM = pl.BlockSpec(memory_space=pltpu.SMEM)
HBM = pl.BlockSpec(memory_space=pltpu.HBM)
VMEM = pl.BlockSpec(memory_space=pltpu.VMEM)


def call(kernel, out_shape, in_specs, scratch=(), cost=None):
    return pl.pallas_call(
        kernel,
        out_shape=out_shape,
        in_specs=in_specs,
        out_specs=jax.tree.map(lambda _: VMEM, out_shape),
        scratch_shapes=list(scratch),
        cost_estimate=cost,
        compiler_params=pltpu.CompilerParams(vmem_limit_bytes=48 * 1024 * 1024),
    )


def shape(*dims, dtype=F32):
    return jax.ShapeDtypeStruct(dims, dtype)


def lists(*pairs, sems):
    copies = [pltpu.make_async_copy(*pair, sems.at[i]) for i, pair in enumerate(pairs)]
    for copy in copies:
        copy.start()
    return copies


def used(count, k, prod):
    return jnp.where(count > k, prod, 0.0)


def forward(blk, rws, cls, cnt, v_ref, acc_ref):
    count = jnp.broadcast_to(cnt[...], (8, 128))
    acc_ref[...] = jnp.zeros_like(acc_ref)
    for k in range(0, blk.shape[0], 2):
        pair = jnp.concatenate([v_ref[cls[0, 0, k]], v_ref[cls[0, 0, k + 1]]], axis=0)
        a = blk[k : k + 2].reshape(256, 128)
        prod = lax.dot_general(
            pair.astype(BF16), a, (((1,), (1,)), ((), ())), preferred_element_type=F32
        )
        acc_ref[rws[0, 0, k]] += used(count, k, prod[:8, :128])
        acc_ref[rws[0, 0, k + 1]] += used(count, k + 1, prod[8:, 128:])


def backward(blk, rws, cls, cnt, u_ref, accs, out):
    count = jnp.broadcast_to(cnt[...], (8, 128))
    for acc in accs:
        acc[...] = jnp.zeros_like(acc)
    zero = jnp.zeros((8, 128), F32)
    for k in range(0, blk.shape[0], 2):
        u0 = jnp.concatenate([u_ref[rws[0, 0, k]], zero], axis=0).astype(BF16)
        u1 = jnp.concatenate([zero, u_ref[rws[0, 0, k + 1]]], axis=0).astype(BF16)
        a = blk[k : k + 2].reshape(256, 128)
        prod = jnp.dot(jnp.concatenate([u0, u1], axis=1), a, preferred_element_type=F32)
        accs[k % len(accs)][cls[0, 0, k]] += used(count, k, prod[:8])
        accs[(k + 1) % len(accs)][cls[0, 0, k + 1]] += used(count, k + 1, prod[8:])
    for c in range(accs[0].shape[0]):
        out[c] = functools.reduce(jnp.add, [acc[c] for acc in accs])


def column(ref):
    rows = lax.broadcasted_iota(jnp.int32, (8, 128), 0)
    out = jnp.zeros((8, 128), F32)
    for s in range(8):
        out = jnp.where(rows == s, ref[s], out)
    return out


def lane_sum(x):
    return jnp.broadcast_to(jnp.sum(x, axis=1, keepdims=True), (8, 128))


def squares(ref, blocks):
    totals = [jnp.zeros((8, 128), F32)] * 4
    for b in range(blocks):
        totals[b % 4] = totals[b % 4] + ref[b] * ref[b]
    return lane_sum((totals[0] + totals[1]) + (totals[2] + totals[3]))


def store_pairs(acc_ref, outs):
    half = acc_ref.shape[0] // 4
    for b in range(2 * half):
        pair = jnp.concatenate([acc_ref[2 * b], acc_ref[2 * b + 1]], axis=0)
        outs[b // half][b % half] = pair.astype(BF16)


def place_halves(own, other, out_ref):
    half = own.shape[1] // 128
    row = lax.axis_index("row")
    for b in range(half):
        out_ref[row * half + b] = own[:, b * 128 : (b + 1) * 128]
        out_ref[(1 - row) * half + b] = other[:, b * 128 : (b + 1) * 128]


def load(own_hbm, own, sem):
    copy = pltpu.make_async_copy(own_hbm, own, sem)
    copy.start()
    copy.wait()


def first_forward(
    rws_ref, cls_ref, cnt, blk, alpha_ref, own, other, u_piece,
    out0, out1, v_out,
    rws, cls, sems, alpha, acc,
):
    copies = lists((rws_ref, rws), (cls_ref, cls), (alpha_ref, alpha), sems=sems)
    place_halves(own, other, v_out)
    for c in copies:
        c.wait()
    forward(blk, rws, cls, cnt, v_out, acc)
    pieces = u_piece.shape[1] // 128
    base = lax.axis_index("col") * pieces
    a = column(alpha)
    for b in range(pieces):
        acc[base + b] -= a * u_piece[:, b * 128 : (b + 1) * 128]
    store_pairs(acc, (out0, out1))


def pair_sums(pairs, a0, a1, b0, b1):
    half = pairs // 2
    for b in range(pairs):
        one, two = (a0, a1) if b < half else (b0, b1)
        yield one[b % half].astype(F32) + two[b % half].astype(F32)


def first_backward(rws_ref, cls_ref, cnt, blk, sums0, sums1, sums2, sums3, upd, message, rws, cls, sems, *accs):
    copies = lists((rws_ref, rws), (cls_ref, cls), sems=sems)
    blocks = upd.shape[0]
    for b, s in enumerate(pair_sums(blocks // 2, sums0, sums1, sums2, sums3)):
        upd[2 * b] = s[:8]
        upd[2 * b + 1] = s[8:]
    cells = message.shape[0] - 1
    message[cells] = squares(upd, blocks)
    for c in copies:
        c.wait()
    backward(blk, rws, cls, cnt, upd, accs, message)


def next_forward(
    total_rays,
    rws_ref, cls_ref, cnt, blk, own, other, v_old,
    out0, out1, vupd, beta_out,
    rws, cls, sems, acc,
):
    copies = lists((rws_ref, rws), (cls_ref, cls), sems=sems)
    cells = v_old.shape[0]
    beta = jnp.sqrt((own[cells] + other[cells]) / total_rays + EPS)
    beta_out[...] = beta
    inv = 1.0 / beta
    for b in range(cells):
        vupd[b] = (own[b] + other[b]) * inv - beta * v_old[b]
    rays = acc.shape[0]
    sq = squares(vupd, cells)
    lanes = lax.broadcasted_iota(jnp.int32, (8, 128), 1)
    sq = jnp.where(lanes == lax.axis_index("col"), sq, 0.0)
    high = sq.astype(BF16).astype(F32)
    out0[rays // 4] = jnp.concatenate([high, sq - high], axis=0).astype(BF16)
    for c in copies:
        c.wait()
    forward(blk, rws, cls, cnt, vupd, acc)
    store_pairs(acc, (out0, out1))


def next_backward(
    total_cells, pieces,
    rws_ref, cls_ref, cnt, blk, sums0, sums1, sums2, sums3, old, beta,
    message, u_piece, alpha_out,
    rws, cls, sems, upd, *accs,
):
    copies = lists((rws_ref, rws), (cls_ref, cls), sems=sems)
    blocks = upd.shape[0]
    tail = sums0[blocks // 4].astype(F32) + sums1[blocks // 4].astype(F32)
    alpha = jnp.sqrt(lane_sum(tail[:8] + tail[8:]) / total_cells + EPS)
    alpha_out[...] = alpha
    inv = 1.0 / alpha
    ratio = alpha / beta[...]
    for b, s in enumerate(pair_sums(blocks // 2, sums0, sums1, sums2, sums3)):
        upd[2 * b] = s[:8] * inv - ratio * old[2 * b]
        upd[2 * b + 1] = s[8:] * inv - ratio * old[2 * b + 1]
    cells = message.shape[0] - 1
    message[cells] = squares(upd, blocks)
    base = lax.axis_index("col") * pieces
    for b in range(pieces):
        u_piece[b] = upd[base + b]
    for c in copies:
        c.wait()
    backward(blk, rws, cls, cnt, upd, accs, message)


def last_cells(total_rays, own, other, v_old, alpha, sq, vupd, beta_out):
    cells = v_old.shape[0]
    beta = jnp.sqrt((own[cells] + other[cells]) / total_rays + EPS)
    beta_out[...] = beta
    inv = 1.0 / beta
    scale = beta / alpha[...]
    for b in range(cells):
        vupd[b] = (own[b] + other[b]) * inv - scale * v_old[b]
    sq[...] = squares(vupd, cells)


def settle(
    phibar_in, rhobar_in, v1, u_piece, x_in, w_in, beta1, alpha1, beta2,
    u_out, x_out, w_mid, factors,
):
    phibar, rhobar, beta, alpha = column(phibar_in), column(rhobar_in), beta1[...], alpha1[...]
    rho = jnp.sqrt(rhobar * rhobar + beta * beta)
    cosine, sine = rhobar / rho, beta / rho
    along, back, inv = cosine * phibar / rho, sine * alpha / rho, 1.0 / alpha
    rhobar, phibar = -cosine * alpha, sine * phibar
    beta = beta2[...]
    rho = jnp.sqrt(rhobar * rhobar + beta * beta)
    cosine, sine = rhobar / rho, beta / rho
    along2 = cosine * phibar / rho
    factors[0], factors[1], factors[2] = sine / rho, -cosine, sine * phibar
    half = x_in.shape[1] // 128
    base = lax.axis_index("row") * half
    for b in range(half):
        at = slice(b * 128, (b + 1) * 128)
        w_old = w_in[:, at]
        w = v1[base + b] * inv - back * w_old
        x_out[:, at] = x_in[:, at] + along * w_old + along2 * w
        w_mid[:, at] = w
    inv = 1.0 / beta
    for b in range(u_piece.shape[0]):
        u_out[:, b * 128 : (b + 1) * 128] = u_piece[b] * inv


def finish(total_cells, sq, v2, w_mid, factors, v_out, w_out, scalars):
    alpha = jnp.sqrt(sq[...] / total_cells + EPS)
    inv, back = 1.0 / alpha, factors[0] * alpha
    half = v_out.shape[1] // 128
    base = lax.axis_index("row") * half
    for b in range(half):
        at = slice(b * 128, (b + 1) * 128)
        v = v2[base + b] * inv
        v_out[:, at], w_out[:, at] = v, v - back * w_mid[:, at]
    rows = lax.broadcasted_iota(jnp.int32, (8, 128), 0)
    lanes = lax.broadcasted_iota(jnp.int32, (8, 128), 1)
    for i, value in enumerate((alpha, factors[2], factors[1] * alpha)):
        line = jnp.sum(jnp.where(rows == lanes, value, 0.0), axis=0, keepdims=True)
        scalars[i : i + 1, :] = line[:, :8]


def other_core(x):
    return lax.ppermute(x, "row", [(0, 1), (1, 0)])


def column_sum(halves):
    n = lax.axis_size("col")
    steps = [1 << i for i in range((n - 1).bit_length())]
    back = steps[::-1]
    orders = (
        (steps[1::-1] + steps[2:], back),
        (steps[:-2] + back[:2], back),
    )
    xs = list(halves)
    for i in range(len(steps)):
        ys = [
            lax.ppermute(
                x,
                ("row", "col"),
                [(j, j ^ first[i]) for j in range(n)] + [(n + j, n + (j ^ second[i])) for j in range(n)],
            )
            for x, (first, second) in zip(xs, orders)
        ]
        if i == len(steps) - 1:
            return xs[0], ys[0], xs[1], ys[1]
        xs = [(x.astype(F32) + y.astype(F32)).astype(BF16) for x, y in zip(xs, ys)]


def last_sum(x):
    n = lax.axis_size("col")
    m = 1
    while m < n:
        pairs = [(i + n * r, (i ^ m) + n * (1 - r)) for r in (0, 1) for i in range(n)]
        x = x + lax.ppermute(x, ("row", "col"), pairs)
        m *= 2
    return x


def body(
    blocks, block_rows, block_cols, counts, u_rays, v_cells, x_cells, w_cells, alpha, phibar, rhobar
):
    n_row = lax.axis_size("row")
    n_col = lax.axis_size("col")
    pieces = u_rays.shape[1] // 128
    half = v_cells.shape[1] // 128
    rays = pieces * n_col
    cells = half * n_row
    total_rays = float(rays * 128 * n_row)
    total_cells = float(cells * 128 * n_col)
    where = (block_rows, block_cols, counts)
    listed = [
        pltpu.SMEM(block_rows.shape, jnp.int32),
        pltpu.SMEM(block_cols.shape, jnp.int32),
        pltpu.SemaphoreType.DMA((3,)),
    ]
    ray_acc = pltpu.VMEM((rays, 8, 128), F32)
    cell_accs = [pltpu.VMEM((cells, 8, 128), F32)] * 4
    own = call(
        load,
        shape(*v_cells.shape),
        [HBM],
        [pltpu.SemaphoreType.DMA],
        pl.CostEstimate(flops=5 * 10**9, bytes_accessed=1, transcendentals=0),
    )(v_cells)
    v_other = other_core(own)
    blk = blocks.reshape(blocks.shape[2:])
    operator = (*where, blk)
    half_rays = shape(rays // 4, 16, 128, dtype=BF16)
    *part, v0 = call(
        first_forward,
        (half_rays, half_rays, shape(cells, 8, 128)),
        [VMEM] * 8,
        listed + [pltpu.SMEM(alpha.shape, F32), ray_acc],
    )(*operator, alpha, own, v_other, u_rays)
    sums = column_sum(part)
    upd1, message = call(
        first_backward,
        (shape(rays, 8, 128), shape(cells + 1, 8, 128)),
        [VMEM] * 8,
        listed + cell_accs,
    )(*operator, *sums)
    *part, v1, beta1 = call(
        functools.partial(next_forward, total_rays),
        (shape(rays // 4 + 1, 16, 128, dtype=BF16), half_rays, shape(cells, 8, 128), shape(8, 128)),
        [VMEM] * 7,
        listed + [ray_acc],
    )(*operator, message, other_core(message), v0)
    sums = column_sum(part)
    message, u_piece, alpha1 = call(
        functools.partial(next_backward, total_cells, pieces),
        (shape(cells + 1, 8, 128), shape(pieces, 8, 128), shape(8, 128)),
        [VMEM] * 10,
        listed + [pltpu.VMEM((rays, 8, 128), F32)] + cell_accs,
    )(*operator, *sums, upd1, beta1)
    sq, v2, beta2 = call(
        functools.partial(last_cells, total_rays),
        (shape(8, 128), shape(cells, 8, 128), shape(8, 128)),
        [VMEM] * 4,
    )(message, other_core(message), v1, alpha1)
    sq = last_sum(sq)
    flat = shape(*v_cells.shape)
    u, x, w_mid, factors = call(
        settle,
        (shape(*u_rays.shape), flat, flat, shape(3, 8, 128)),
        [SMEM] * 2 + [VMEM] * 7,
        (),
        pl.CostEstimate(flops=10**6, bytes_accessed=3 * 10**6, transcendentals=0),
    )(phibar, rhobar, v1, u_piece, x_cells, w_cells, beta1, alpha1, beta2)
    v, w, scalars = call(
        functools.partial(finish, total_cells), (flat, flat, shape(3, 8)), [VMEM] * 4
    )(sq, v2, w_mid, factors)
    return u, v, x, w, scalars


def solution(mesh):
    placed = (
        P(("region", "row"), "col", None, None, None),
        P(("region", "row"), "col", None),
        P(("region", "row"), "col", None),
        P(("region", "row"), "col"),
        P(None, ("region", "row", "col")),
        P(None, ("region", "col", "row")),
        P(None, ("region", "col", "row")),
        P(None, ("region", "col", "row")),
        P("region"),
        P("region"),
        P("region"),
    )
    return jax.shard_map(
        body,
        mesh=mesh,
        in_specs=placed,
        out_specs=(
            P(None, ("region", "row", "col")),
            P(None, ("region", "col", "row")),
            P(None, ("region", "col", "row")),
            P(None, ("region", "col", "row")),
            P(None, "region"),
        ),
        check_vma=False,
    )
```

```python
import functools

import jax
import jax.numpy as jnp
from jax import lax
from jax.experimental import pallas as pl
from jax.experimental.pallas import tpu as pltpu
from jax.sharding import PartitionSpec as P

ITERS = 2
EPS = 1e-6
F32 = jnp.float32
BF16 = jnp.bfloat16
SMEM = pl.BlockSpec(memory_space=pltpu.SMEM)
HBM = pl.BlockSpec(memory_space=pltpu.HBM)
VMEM = pl.BlockSpec(memory_space=pltpu.VMEM)


def call(kernel, out_shape, in_specs, scratch=(), cost=None):
    return pl.pallas_call(
        kernel,
        out_shape=out_shape,
        in_specs=in_specs,
        out_specs=jax.tree.map(lambda _: VMEM, out_shape),
        scratch_shapes=list(scratch),
        cost_estimate=cost,
        compiler_params=pltpu.CompilerParams(vmem_limit_bytes=48 * 1024 * 1024),
    )


def shape(*dims, dtype=F32):
    return jax.ShapeDtypeStruct(dims, dtype)


def lists(*pairs, sems):
    copies = [pltpu.make_async_copy(*pair, sems.at[i]) for i, pair in enumerate(pairs)]
    for copy in copies:
        copy.start()
    return copies


def used(count, k, prod):
    return jnp.where(count > k, prod, 0.0)


def forward(blk, rws, cls, cnt, v_ref, acc_ref):
    count = jnp.broadcast_to(cnt[...], (8, 128))
    acc_ref[...] = jnp.zeros_like(acc_ref)
    for k in range(0, blk.shape[0], 2):
        pair = jnp.concatenate([v_ref[cls[0, 0, k]], v_ref[cls[0, 0, k + 1]]], axis=0)
        a = blk[k : k + 2].reshape(256, 128)
        prod = lax.dot_general(
            pair.astype(BF16), a, (((1,), (1,)), ((), ())), preferred_element_type=F32
        )
        acc_ref[rws[0, 0, k]] += used(count, k, prod[:8, :128])
        acc_ref[rws[0, 0, k + 1]] += used(count, k + 1, prod[8:, 128:])


def backward(blk, rws, cls, cnt, u_ref, accs, out):
    count = jnp.broadcast_to(cnt[...], (8, 128))
    for acc in accs:
        acc[...] = jnp.zeros_like(acc)
    zero = jnp.zeros((8, 128), F32)
    for k in range(0, blk.shape[0], 2):
        u0 = jnp.concatenate([u_ref[rws[0, 0, k]], zero], axis=0).astype(BF16)
        u1 = jnp.concatenate([zero, u_ref[rws[0, 0, k + 1]]], axis=0).astype(BF16)
        a = blk[k : k + 2].reshape(256, 128)
        prod = jnp.dot(jnp.concatenate([u0, u1], axis=1), a, preferred_element_type=F32)
        accs[k % len(accs)][cls[0, 0, k]] += used(count, k, prod[:8])
        accs[(k + 1) % len(accs)][cls[0, 0, k + 1]] += used(count, k + 1, prod[8:])
    for c in range(accs[0].shape[0]):
        out[c] = functools.reduce(jnp.add, [acc[c] for acc in accs])


def column(ref):
    rows = lax.broadcasted_iota(jnp.int32, (8, 128), 0)
    out = jnp.zeros((8, 128), F32)
    for s in range(8):
        out = jnp.where(rows == s, ref[s], out)
    return out


def lane_sum(x):
    return jnp.broadcast_to(jnp.sum(x, axis=1, keepdims=True), (8, 128))


def squares(ref, blocks):
    totals = [jnp.zeros((8, 128), F32)] * 4
    for b in range(blocks):
        totals[b % 4] = totals[b % 4] + ref[b] * ref[b]
    return lane_sum((totals[0] + totals[1]) + (totals[2] + totals[3]))


def store_pairs(acc_ref, outs):
    half = acc_ref.shape[0] // 4
    for b in range(2 * half):
        pair = jnp.concatenate([acc_ref[2 * b], acc_ref[2 * b + 1]], axis=0)
        outs[b // half][b % half] = pair.astype(BF16)


def place_halves(own, other, out_ref):
    half = own.shape[1] // 128
    row = lax.axis_index("row")
    for b in range(half):
        out_ref[row * half + b] = own[:, b * 128 : (b + 1) * 128]
        out_ref[(1 - row) * half + b] = other[:, b * 128 : (b + 1) * 128]


def load(own_hbm, own, sem):
    copy = pltpu.make_async_copy(own_hbm, own, sem)
    copy.start()
    copy.wait()


def first_forward(
    rws_ref, cls_ref, cnt, blk, alpha_ref, own, other, u_piece,
    out0, out1, v_out,
    rws, cls, sems, alpha, acc,
):
    copies = lists((rws_ref, rws), (cls_ref, cls), (alpha_ref, alpha), sems=sems)
    place_halves(own, other, v_out)
    for c in copies:
        c.wait()
    forward(blk, rws, cls, cnt, v_out, acc)
    pieces = u_piece.shape[1] // 128
    base = lax.axis_index("col") * pieces
    a = column(alpha)
    for b in range(pieces):
        acc[base + b] -= a * u_piece[:, b * 128 : (b + 1) * 128]
    store_pairs(acc, (out0, out1))


def pair_sums(pairs, a0, a1, b0, b1):
    half = pairs // 2
    for b in range(pairs):
        one, two = (a0, a1) if b < half else (b0, b1)
        yield one[b % half].astype(F32) + two[b % half].astype(F32)


def first_backward(rws_ref, cls_ref, cnt, blk, sums0, sums1, sums2, sums3, upd, message, rws, cls, sems, *accs):
    copies = lists((rws_ref, rws), (cls_ref, cls), sems=sems)
    blocks = upd.shape[0]
    for b, s in enumerate(pair_sums(blocks // 2, sums0, sums1, sums2, sums3)):
        upd[2 * b] = s[:8]
        upd[2 * b + 1] = s[8:]
    cells = message.shape[0] - 1
    message[cells] = squares(upd, blocks)
    for c in copies:
        c.wait()
    backward(blk, rws, cls, cnt, upd, accs, message)


def next_forward(
    total_rays,
    rws_ref, cls_ref, cnt, blk, own, other, v_old,
    out0, out1, vupd, beta_out,
    rws, cls, sems, acc,
):
    copies = lists((rws_ref, rws), (cls_ref, cls), sems=sems)
    cells = v_old.shape[0]
    beta = jnp.sqrt((own[cells] + other[cells]) / total_rays + EPS)
    beta_out[...] = beta
    inv = 1.0 / beta
    for b in range(cells):
        vupd[b] = (own[b] + other[b]) * inv - beta * v_old[b]
    rays = acc.shape[0]
    sq = squares(vupd, cells)
    lanes = lax.broadcasted_iota(jnp.int32, (8, 128), 1)
    sq = jnp.where(lanes == lax.axis_index("col"), sq, 0.0)
    high = sq.astype(BF16).astype(F32)
    out0[rays // 4] = jnp.concatenate([high, sq - high], axis=0).astype(BF16)
    for c in copies:
        c.wait()
    forward(blk, rws, cls, cnt, vupd, acc)
    store_pairs(acc, (out0, out1))


def next_backward(
    total_cells, pieces,
    rws_ref, cls_ref, cnt, blk, sums0, sums1, sums2, sums3, old, beta,
    message, u_piece, alpha_out,
    rws, cls, sems, upd, *accs,
):
    copies = lists((rws_ref, rws), (cls_ref, cls), sems=sems)
    blocks = upd.shape[0]
    tail = sums0[blocks // 4].astype(F32) + sums1[blocks // 4].astype(F32)
    alpha = jnp.sqrt(lane_sum(tail[:8] + tail[8:]) / total_cells + EPS)
    alpha_out[...] = alpha
    inv = 1.0 / alpha
    ratio = alpha / beta[...]
    for b, s in enumerate(pair_sums(blocks // 2, sums0, sums1, sums2, sums3)):
        upd[2 * b] = s[:8] * inv - ratio * old[2 * b]
        upd[2 * b + 1] = s[8:] * inv - ratio * old[2 * b + 1]
    cells = message.shape[0] - 1
    message[cells] = squares(upd, blocks)
    base = lax.axis_index("col") * pieces
    for b in range(pieces):
        u_piece[b] = upd[base + b]
    for c in copies:
        c.wait()
    backward(blk, rws, cls, cnt, upd, accs, message)


def last_cells(total_rays, own, other, v_old, alpha, sq, vupd, beta_out):
    cells = v_old.shape[0]
    beta = jnp.sqrt((own[cells] + other[cells]) / total_rays + EPS)
    beta_out[...] = beta
    inv = 1.0 / beta
    scale = beta / alpha[...]
    for b in range(cells):
        vupd[b] = (own[b] + other[b]) * inv - scale * v_old[b]
    sq[...] = squares(vupd, cells)


def settle(
    phibar_in, rhobar_in, v1, u_piece, x_in, w_in, beta1, alpha1, beta2,
    u_out, x_out, w_mid, factors,
):
    phibar, rhobar, beta, alpha = column(phibar_in), column(rhobar_in), beta1[...], alpha1[...]
    rho = jnp.sqrt(rhobar * rhobar + beta * beta)
    cosine, sine = rhobar / rho, beta / rho
    along, back, inv = cosine * phibar / rho, sine * alpha / rho, 1.0 / alpha
    rhobar, phibar = -cosine * alpha, sine * phibar
    beta = beta2[...]
    rho = jnp.sqrt(rhobar * rhobar + beta * beta)
    cosine, sine = rhobar / rho, beta / rho
    along2 = cosine * phibar / rho
    factors[0], factors[1], factors[2] = sine / rho, -cosine, sine * phibar
    half = x_in.shape[1] // 128
    base = lax.axis_index("row") * half
    for b in range(half):
        at = slice(b * 128, (b + 1) * 128)
        w_old = w_in[:, at]
        w = v1[base + b] * inv - back * w_old
        x_out[:, at] = x_in[:, at] + along * w_old + along2 * w
        w_mid[:, at] = w
    inv = 1.0 / beta
    for b in range(u_piece.shape[0]):
        u_out[:, b * 128 : (b + 1) * 128] = u_piece[b] * inv


def finish(total_cells, sq, v2, w_mid, factors, v_out, w_out, scalars):
    alpha = jnp.sqrt(sq[...] / total_cells + EPS)
    inv, back = 1.0 / alpha, factors[0] * alpha
    half = v_out.shape[1] // 128
    base = lax.axis_index("row") * half
    for b in range(half):
        at = slice(b * 128, (b + 1) * 128)
        v = v2[base + b] * inv
        v_out[:, at], w_out[:, at] = v, v - back * w_mid[:, at]
    rows = lax.broadcasted_iota(jnp.int32, (8, 128), 0)
    lanes = lax.broadcasted_iota(jnp.int32, (8, 128), 1)
    for i, value in enumerate((alpha, factors[2], factors[1] * alpha)):
        line = jnp.sum(jnp.where(rows == lanes, value, 0.0), axis=0, keepdims=True)
        scalars[i : i + 1, :] = line[:, :8]


def other_core(x):
    return lax.ppermute(x, "row", [(0, 1), (1, 0)])


def column_sum(halves):
    n = lax.axis_size("col")
    steps = [1 << i for i in range((n - 1).bit_length())]
    back = steps[::-1]
    orders = (
        (steps[1::-1] + steps[2:], back),
        (steps[:-2] + back[:2], back),
    )
    xs = list(halves)
    for i in range(len(steps)):
        ys = [
            lax.ppermute(
                x,
                ("row", "col"),
                [(j, j ^ first[i]) for j in range(n)] + [(n + j, n + (j ^ second[i])) for j in range(n)],
            )
            for x, (first, second) in zip(xs, orders)
        ]
        if i == len(steps) - 1:
            return xs[0], ys[0], xs[1], ys[1]
        xs = [(x.astype(F32) + y.astype(F32)).astype(BF16) for x, y in zip(xs, ys)]


def last_sum(x):
    n = lax.axis_size("col")
    steps = [1 << i for i in range((n - 1).bit_length())]
    for m in steps[1:] + steps[:1]:
        pairs = [(i + n * r, (i ^ m) + n * (1 - r)) for r in (0, 1) for i in range(n)]
        x = x + lax.ppermute(x, ("row", "col"), pairs)
    return x


def body(
    blocks, block_rows, block_cols, counts, u_rays, v_cells, x_cells, w_cells, alpha, phibar, rhobar
):
    n_row = lax.axis_size("row")
    n_col = lax.axis_size("col")
    pieces = u_rays.shape[1] // 128
    half = v_cells.shape[1] // 128
    rays = pieces * n_col
    cells = half * n_row
    total_rays = float(rays * 128 * n_row)
    total_cells = float(cells * 128 * n_col)
    where = (block_rows, block_cols, counts)
    listed = [
        pltpu.SMEM(block_rows.shape, jnp.int32),
        pltpu.SMEM(block_cols.shape, jnp.int32),
        pltpu.SemaphoreType.DMA((3,)),
    ]
    ray_acc = pltpu.VMEM((rays, 8, 128), F32)
    cell_accs = [pltpu.VMEM((cells, 8, 128), F32)] * 4
    own = call(
        load,
        shape(*v_cells.shape),
        [HBM],
        [pltpu.SemaphoreType.DMA],
        pl.CostEstimate(flops=5 * 10**9, bytes_accessed=1, transcendentals=0),
    )(v_cells)
    v_other = other_core(own)
    blk = blocks.reshape(blocks.shape[2:])
    operator = (*where, blk)
    half_rays = shape(rays // 4, 16, 128, dtype=BF16)
    *part, v0 = call(
        first_forward,
        (half_rays, half_rays, shape(cells, 8, 128)),
        [VMEM] * 8,
        listed + [pltpu.SMEM(alpha.shape, F32), ray_acc],
    )(*operator, alpha, own, v_other, u_rays)
    sums = column_sum(part)
    upd1, message = call(
        first_backward,
        (shape(rays, 8, 128), shape(cells + 1, 8, 128)),
        [VMEM] * 8,
        listed + cell_accs,
    )(*operator, *sums)
    *part, v1, beta1 = call(
        functools.partial(next_forward, total_rays),
        (shape(rays // 4 + 1, 16, 128, dtype=BF16), half_rays, shape(cells, 8, 128), shape(8, 128)),
        [VMEM] * 7,
        listed + [ray_acc],
    )(*operator, message, other_core(message), v0)
    sums = column_sum(part)
    message, u_piece, alpha1 = call(
        functools.partial(next_backward, total_cells, pieces),
        (shape(cells + 1, 8, 128), shape(pieces, 8, 128), shape(8, 128)),
        [VMEM] * 10,
        listed + [pltpu.VMEM((rays, 8, 128), F32)] + cell_accs,
    )(*operator, *sums, upd1, beta1)
    sq, v2, beta2 = call(
        functools.partial(last_cells, total_rays),
        (shape(8, 128), shape(cells, 8, 128), shape(8, 128)),
        [VMEM] * 4,
    )(message, other_core(message), v1, alpha1)
    sq = last_sum(sq)
    flat = shape(*v_cells.shape)
    u, x, w_mid, factors = call(
        settle,
        (shape(*u_rays.shape), flat, flat, shape(3, 8, 128)),
        [SMEM] * 2 + [VMEM] * 7,
        (),
        pl.CostEstimate(flops=10**6, bytes_accessed=3 * 10**6, transcendentals=0),
    )(phibar, rhobar, v1, u_piece, x_cells, w_cells, beta1, alpha1, beta2)
    v, w, scalars = call(
        functools.partial(finish, total_cells), (flat, flat, shape(3, 8)), [VMEM] * 4
    )(sq, v2, w_mid, factors)
    return u, v, x, w, scalars


def solution(mesh):
    placed = (
        P(("region", "row"), "col", None, None, None),
        P(("region", "row"), "col", None),
        P(("region", "row"), "col", None),
        P(("region", "row"), "col"),
        P(None, ("region", "row", "col")),
        P(None, ("region", "col", "row")),
        P(None, ("region", "col", "row")),
        P(None, ("region", "col", "row")),
        P("region"),
        P("region"),
        P("region"),
    )
    return jax.shard_map(
        body,
        mesh=mesh,
        in_specs=placed,
        out_specs=(
            P(None, ("region", "row", "col")),
            P(None, ("region", "col", "row")),
            P(None, ("region", "col", "row")),
            P(None, ("region", "col", "row")),
            P(None, "region"),
        ),
        check_vma=False,
    )
```
